256 devices in a mesh: dp: 64 (over y, z, core), mp: 4 (over x).
Axes of the slice: x: 4, y: 4, z: 8, core: 2. Of those that a mesh axis runs over, the one named last changes fastest.
Arguments:
- pixels: bfloat16 [9216, 588], P('dp'), may hold values from -40 to 40
- patch_counts: int32 [192], P('dp'), may hold values from 12 to 48, as said below
- pack_index: int32 [192], P('dp'), may hold values from 0 to 63, as said below
- embed_weight: bfloat16 [588, 4, 1536], P(None, 'mp', 'dp'), may hold values from -1 to 1
- norm_gain: float32 [6144], P('mp'), may hold values from 0.5 to 1.5
- query_weight: bfloat16 [6144, 3072], P('dp', 'mp'), may hold values from -0.078125 to 0.078125
- key_weight: bfloat16 [6144, 3072], P('dp', 'mp'), may hold values from -0.078125 to 0.078125
- query_gain: float32 [128], replicated, may hold values from 0.1 to 1.9
- key_gain: float32 [128], replicated, may hold values from 0.1 to 1.9
- cotangent: bfloat16 [12288, 3072], P('dp', 'mp'), may hold values from -0.0625 to 0.0625
Outputs:
- attended: bfloat16 [12288, 3072], P('dp', 'mp')
- embed_grad: float32 [588, 4, 1536], P(None, 'mp', 'dp')
The draws below stay inside these ranges and needn't reach their ends.
Inputs may be any that keep to these rules, and one draw needn't show every extreme that they name: `patch_counts`: each draw has 4 images of 48 patches in one pack. `pack_index`: the pack of an image held by loader l is l plus one of 0 to 3, modulo the length of the dp axis; the images of one loader go to different packs.
All inputs are finite; a program needn't handle non-finite values.
Results may differ from the reference program's by a relative error of at most 0.015.
Values may be sent and summed in bfloat16 or wider, within the bound.
No kernel may reach another device: no remote copies, remote signals or barrier semaphores. Data moves between devices by JAX's collectives and lax.ppermute only.
A program may use at most 128 MiB of HBM per device.

```python
import jax
import jax.numpy as jnp
from jax import lax

D = 6144
HEADS = 24
HD = 128
PATCH = 588
MOST = 48
IMG_LOAD = 3
REACH = 4
FEAT = 1536
IMAGES = 192
ROWS = 12288
N_DP = 64
N_MP = 4


def route_tables(key):
    key_order, key_length, key_pick = jax.random.split(key, 3)
    ranking = jax.random.randint(key_order, (N_DP, REACH), 0, 1 << 20) * REACH + jnp.arange(REACH, dtype=jnp.int32)[None, :]
    order = jnp.argsort(ranking, axis=1).astype(jnp.int32)
    lengths = jax.random.randint(key_length, (N_DP, IMG_LOAD), MOST // 4, MOST + 1)
    chosen = jax.random.randint(key_pick, (), 0, N_DP)
    loaders = jnp.arange(N_DP, dtype=jnp.int32)
    distance = (chosen - loaders) % N_DP
    forced = distance < REACH
    rotated = (order - order[:, :1] + distance[:, None]) % REACH
    order = jnp.where(forced[:, None], rotated, order)
    lengths = lengths.at[:, 0].set(jnp.where(forced, MOST, lengths[:, 0]))
    packs = (loaders[:, None] + order[:, :IMG_LOAD]) % N_DP
    return (lengths.reshape(-1).astype(jnp.int32), packs.reshape(-1).astype(jnp.int32))


def draw_patch_counts(key, part):
    return route_tables(key)[0]


def draw_pack_index(key, part):
    return route_tables(key)[1]


def draw_pixels(key, part):
    key = jax.random.fold_in(key, 11)
    key_noise, key_rows, key_cols = jax.random.split(key, 3)
    noise_rows = jnp.clip(jax.random.normal(key_noise, (IMAGES * MOST, PATCH), jnp.float32), -6.0, 6.0)
    row_scale = jnp.exp(jax.random.uniform(key_rows, (IMAGES * MOST, 1), jnp.float32, -1.15, 1.15))
    col_scale = jnp.exp(jax.random.uniform(key_cols, (1, PATCH), jnp.float32, -0.35, 0.35))
    return (noise_rows * row_scale * col_scale).astype(jnp.bfloat16)


def draw_embed_weight(key, part):
    key = jax.random.fold_in(key, 23)
    columns = jnp.arange(D, dtype=jnp.float32).reshape(1, D // FEAT, FEAT)
    noise_cols = jnp.clip(jax.random.normal(key, (PATCH, D // FEAT, FEAT), jnp.float32), -6.0, 6.0)
    growth = 1.1
    profile = jnp.exp(growth * columns / D)
    scaled = jnp.clip(noise_cols * profile * PATCH ** (-0.5), -1.0, 1.0)
    return scaled.astype(jnp.bfloat16)


def block_levels(stream_key, dims, pieces, low, top_value):
    level = 1.0
    for axis_at, shards_of in pieces:
        heights = jax.random.uniform(jax.random.fold_in(jax.random.fold_in(stream_key, 6), axis_at), (shards_of,), jnp.float32, low / len(pieces), top_value / len(pieces))
        level = level * jnp.repeat(jnp.exp(heights), dims[axis_at] // shards_of).reshape((-1,) + (1,) * (len(dims) - 1 - axis_at))
    return level


def bell_draw(own_key, extent, scale, most, shards=(), kind=jnp.bfloat16):
    gain = block_levels(own_key, extent, shards, -0.22, 0.18) if shards else 1.0
    entries = jax.random.normal(own_key, extent, jnp.float32) * scale * gain
    return jnp.minimum(jnp.maximum(entries, -most), most).astype(kind)


def setup_inputs(seed: int = 0) -> dict:
    streams_of = jax.random.split(jax.random.key(seed), 11)
    return {
        "pixels": draw_pixels(jax.random.fold_in(streams_of[10], 71), 0),
        "patch_counts": draw_patch_counts(jax.random.fold_in(streams_of[10], 71), 0),
        "pack_index": draw_pack_index(jax.random.fold_in(streams_of[10], 71), 0),
        "embed_weight": draw_embed_weight(jax.random.fold_in(streams_of[10], 71), 0),
        "norm_gain": jnp.clip(1.0 + 0.1 * jax.random.normal(streams_of[4], (D,), jnp.float32), 0.5, 1.5),
        "query_weight": bell_draw(streams_of[5], (D, HEADS * HD), D ** -0.5, 0.078125, ((0, 64), (1, 4))),
        "key_weight": bell_draw(streams_of[6], (D, HEADS * HD), D ** -0.5, 0.078125, ((0, 64), (1, 4))),
        "query_gain": jnp.clip(1.0 + 0.18 * jax.random.normal(streams_of[7], (HD,), jnp.float32), 0.1, 1.9),
        "key_gain": jnp.clip(1.0 + 0.18 * jax.random.normal(streams_of[8], (HD,), jnp.float32), 0.1, 1.9),
        "cotangent": bell_draw(streams_of[9], (ROWS, HEADS * HD), 0.01, 0.0625, ((0, 64), (1, 4))),
    }


EPS = 1e-06

def head_norm(values, heads_here, head_size):
    shaped = values.reshape(values.shape[0], heads_here, head_size)
    center = lax.optimization_barrier(jnp.mean(shaped, axis=2, keepdims=True))
    spread = lax.optimization_barrier(jnp.mean(shaped * shaped, axis=2, keepdims=True)) - center * center
    inv_spread = lax.rsqrt(spread + EPS)
    return ((shaped - center) * inv_spread, inv_spread)

def head_back(grad_hat, unit_rows, inv_spread, gain_vec):
    grad_unit = grad_hat * gain_vec
    mean_grad = lax.optimization_barrier(jnp.mean(grad_unit, axis=2, keepdims=True))
    second = lax.optimization_barrier(jnp.mean(grad_unit * unit_rows, axis=2, keepdims=True))
    return inv_spread * (grad_unit - mean_grad - unit_rows * second)

def attend(query_hat, key_hat, values, grad_out, segment, live_rows, head_size):
    query_f = query_hat.astype(jnp.float32)
    key_f = key_hat.astype(jnp.float32)
    values_f = values.astype(jnp.float32)
    grad_f = grad_out.astype(jnp.float32)
    scores = jnp.einsum('bihd,bjhd->bhij', query_f, key_f) * head_size ** (-0.5)
    allowed = (segment[:, :, None] == segment[:, None, :]) & live_rows[:, :, None] & live_rows[:, None, :]
    raised = jnp.where(allowed[:, None], jnp.exp(scores), jnp.zeros_like(scores))
    totals = lax.optimization_barrier(jnp.sum(raised, axis=3, keepdims=True))
    totals = jnp.where(live_rows[:, None, :, None], totals, jnp.ones_like(totals))
    attn_probs = raised / totals
    attn_low = attn_probs.astype(jnp.bfloat16).astype(jnp.float32)
    blended = jnp.einsum('bhij,bjhg->bihg', attn_low, values_f)
    grad_probs = jnp.einsum('bihg,bjhg->bhij', grad_f, values_f)
    grad_values = jnp.einsum('bhij,bihg->bjhg', attn_low, grad_f)
    grad_scores = attn_probs * (grad_probs - lax.optimization_barrier(jnp.sum(attn_probs * grad_probs, axis=3, keepdims=True)))
    grad_low = (grad_scores * head_size ** (-0.5)).astype(jnp.bfloat16).astype(jnp.float32)
    grad_query = jnp.einsum('bhij,bjhd->bihd', grad_low, key_f)
    grad_key = jnp.einsum('bhij,bihd->bjhd', grad_low, query_f)
    return (blended, grad_values, grad_query, grad_key)

def reference(pixels, patch_counts, pack_index, embed_weight, norm_gain, query_weight, key_weight, query_gain, key_gain, cotangent):
    pack_rows = REACH * MOST
    group_width = D // HEADS
    loader_of = jnp.arange(IMAGES, dtype=jnp.int32) // IMG_LOAD
    slot_of = (pack_index - loader_of) % N_DP
    positions = jnp.arange(MOST, dtype=jnp.int32)
    source_live = positions[None, :] < patch_counts[:, None]
    source = pixels.reshape(IMAGES, MOST, PATCH)
    source = jnp.where(source_live[:, :, None], source, jnp.zeros_like(source))
    targets = ((pack_index * REACH + slot_of) * MOST)[:, None] + positions[None, :]
    packed = jnp.zeros((N_DP * pack_rows, PATCH), pixels.dtype).at[targets.reshape(-1)].set(source.reshape(IMAGES * MOST, PATCH))
    slot_counts = jnp.zeros((N_DP * REACH,), jnp.int32).at[pack_index * REACH + slot_of].set(patch_counts)
    embed_flat = embed_weight.reshape(PATCH, D)
    segment = (jnp.arange(pack_rows, dtype=jnp.int32) // MOST)[None, :]
    gain_row = norm_gain.astype(jnp.float32)
    query_gain_f = query_gain.astype(jnp.float32)
    key_gain_f = key_gain.astype(jnp.float32)
    contract = (((1,), (1,)), ((), ()))
    contract_rows = (((0,), (0,)), ((), ()))

    def one_pack(grad_total, inputs):
        patches, counts, grad_in = inputs
        live_rows = (positions[None, :] < counts[:, None]).reshape(1, pack_rows)
        embedded = jnp.dot(patches, embed_flat, preferred_element_type=jnp.float32).astype(jnp.bfloat16)
        wide_rows = embedded.astype(jnp.float32)
        row_mean = lax.optimization_barrier(jnp.mean(wide_rows, axis=1, keepdims=True))
        row_var = lax.optimization_barrier(jnp.mean(wide_rows * wide_rows, axis=1, keepdims=True)) - row_mean * row_mean
        row_scale = lax.rsqrt(row_var + EPS)
        unit_rows = (wide_rows - row_mean) * row_scale
        normed = (unit_rows * gain_row).astype(jnp.bfloat16)
        queries = jnp.dot(normed, query_weight, preferred_element_type=jnp.float32)
        key_rows = jnp.dot(normed, key_weight, preferred_element_type=jnp.float32)
        query_unit, query_scale = head_norm(queries, HEADS, HD)
        key_unit, key_scale = head_norm(key_rows, HEADS, HD)
        query_hat = (query_unit * query_gain_f).astype(jnp.bfloat16)
        key_hat = (key_unit * key_gain_f).astype(jnp.bfloat16)
        values = normed.reshape(1, pack_rows, HEADS, group_width)[:, :, :, :HD]
        grad_out = grad_in.reshape(1, pack_rows, HEADS, HD)
        blended, grad_values, grad_query, grad_key = attend(query_hat.reshape(1, pack_rows, HEADS, HD), key_hat.reshape(1, pack_rows, HEADS, HD), values, grad_out, segment, live_rows, HD)
        attended = blended.reshape(pack_rows, HEADS * HD).astype(jnp.bfloat16)
        grad_values = grad_values.reshape(pack_rows, HEADS, HD)
        grad_values = jnp.concatenate([grad_values, jnp.zeros((pack_rows, HEADS, group_width - HD), jnp.float32)], axis=2)
        grad_query = head_back(grad_query.reshape(pack_rows, HEADS, HD), query_unit, query_scale, query_gain_f)
        grad_key = head_back(grad_key.reshape(pack_rows, HEADS, HD), key_unit, key_scale, key_gain_f)
        query_low = grad_query.reshape(pack_rows, HEADS * HD).astype(jnp.bfloat16)
        key_low = grad_key.reshape(pack_rows, HEADS * HD).astype(jnp.bfloat16)
        grad_normed = lax.dot_general(query_low, query_weight, contract, preferred_element_type=jnp.float32)
        grad_normed = grad_normed + lax.dot_general(key_low, key_weight, contract, preferred_element_type=jnp.float32)
        grad_normed = grad_normed + grad_values.reshape(pack_rows, D)
        grad_unit = grad_normed * gain_row
        mean_grad = lax.optimization_barrier(jnp.mean(grad_unit, axis=1, keepdims=True))
        cross_mean = lax.optimization_barrier(jnp.mean(grad_unit * unit_rows, axis=1, keepdims=True))
        grad_embedded = (row_scale * (grad_unit - mean_grad - unit_rows * cross_mean)).astype(jnp.bfloat16)
        grad_total = grad_total + lax.dot_general(patches, grad_embedded, contract_rows, preferred_element_type=jnp.float32)
        return (grad_total, attended)
    grad_total, attended = lax.scan(one_pack, jnp.zeros((PATCH, D), jnp.float32), (packed.reshape(N_DP, pack_rows, PATCH), slot_counts.reshape(N_DP, REACH), cotangent.reshape(N_DP, pack_rows, HEADS * HD)))
    return (attended.reshape(N_DP * pack_rows, HEADS * HD), grad_total.reshape(PATCH, N_MP, D // N_MP))
```

```python
import jax
import jax.numpy as jnp
from jax import lax
from jax.experimental import pallas as pl
from jax.experimental.pallas import tpu as pltpu
from jax.sharding import PartitionSpec as P

D = 6144
HEADS = 24
HD = 128
PATCH = 588
MOST = 48
IMG_LOAD = 3
REACH = 4
EPS = 1e-06

NY, NZ, NC, NX = 4, 8, 2, 4
NDP = NY * NZ * NC
FX = D // NX
FB = FX // NC
HC = HEADS // NX // NC
HW = HC * HD
ROWS = NC * IMG_LOAD * MOST
EROWS = ROWS + 16
STRIP = FB // NZ
PACK = REACH * MOST
PIECE = FX // NDP
YROWS = NZ * PIECE
NT = (((1,), (1,)), ((), ()))
TN = (((0,), (0,)), ((), ()))
F32 = jnp.float32
BF16 = jnp.bfloat16
HIGH = lax.Precision.HIGHEST


def dot(a, b, dims=(((1,), (0,)), ((), ()))):
    return lax.dot_general(a, b, dims, preferred_element_type=F32)


def dp_index(y, z, c):
    return ((y % NY) * NZ + z % NZ) * NC + c


DP_ALL = [(y, z, c) for y in range(NY) for z in range(NZ) for c in range(NC)]


def core_swap(v):
    return lax.ppermute(v, "dp", [(i, i ^ 1) for i in range(NDP)])


def z_shift(v, k):
    return lax.ppermute(v, "dp", [(dp_index(y, z, c), dp_index(y, z + k, c)) for y, z, c in DP_ALL])


def y_shift(v, k):
    return lax.ppermute(v, "dp", [(dp_index(y, z, c), dp_index(y + k, z, c)) for y, z, c in DP_ALL])


def x_shift(v, k):
    return lax.ppermute(v, "mp", [(i, (i + k) % NX) for i in range(NX)])


def chip_shift(v, k):
    return lax.ppermute(v, "dp", [(i, (i + NC * k) % NDP) for i in range(NDP)])


def by_core(core, mine, other, axis):
    return jnp.where(
        core == 0,
        jnp.concatenate([mine, other], axis=axis),
        jnp.concatenate([other, mine], axis=axis),
    )


def turn(pieces, start, axis):
    n = len(pieces)
    double = jnp.concatenate(list(pieces) + list(pieces), axis=axis)
    size = pieces[0].shape[axis]
    return lax.dynamic_slice_in_dim(double, start * size, n * size, axis=axis)


def vmem(n):
    return [pl.BlockSpec(memory_space=pltpu.VMEM)] * n


def embed_kernel(place, pix, w0, w1, w2, w3, gain, out, weights):
    y = place[1]
    for k, piece in enumerate((w0, w1, w2, w3)):
        at = pl.multiple_of(lax.rem(y + k, NY) * YROWS, YROWS)
        weights[pl.ds(at, YROWS), :] = piece[...]
    out[:ROWS, :] = dot(pix[...], weights[...], NT).astype(BF16)
    full = gain[...]
    high = full.astype(BF16)
    rest = full - high.astype(F32)
    mid = rest.astype(BF16)
    low = (rest - mid.astype(F32)).astype(BF16)
    row = lax.broadcasted_iota(jnp.int32, (16, FB), 0)
    out[ROWS:, :] = jnp.where(
        row == 0,
        high.astype(F32),
        jnp.where(row == 1, mid.astype(F32), jnp.where(row == 2, low.astype(F32), 0.0)),
    ).astype(BF16)


def embed(place, pix, pieces, gain):
    return pl.pallas_call(
        embed_kernel,
        out_shape=jax.ShapeDtypeStruct((EROWS, FB), BF16),
        in_specs=[pl.BlockSpec(memory_space=pltpu.SMEM)] + vmem(6),
        out_specs=pl.BlockSpec(memory_space=pltpu.VMEM),
        scratch_shapes=[pltpu.VMEM((FB, PATCH), BF16)],
        compiler_params=pltpu.CompilerParams(vmem_limit_bytes=24 * 2**20),
        cost_estimate=pl.CostEstimate(
            flops=2 * ROWS * FB * PATCH, bytes_accessed=2000000, transcendentals=0
        ),
        name="embed",
    )(place, pix, *pieces, gain)


def gain_of(rows):
    wide = rows.astype(F32)
    return wide[0:1] + wide[1:2] + wide[2:3]


def head_norm(values):
    center = jnp.mean(values, axis=1, keepdims=True)
    spread = jnp.mean(values * values, axis=1, keepdims=True) - center * center
    inv = lax.rsqrt(spread + EPS)
    return (values - center) * inv, inv


def head_back(grad_hat, unit, inv, gain):
    t = grad_hat * gain
    mean_t = jnp.mean(t, axis=1, keepdims=True)
    second = jnp.mean(t * unit, axis=1, keepdims=True)
    return inv * (t - mean_t - unit * second)


def lanes_sum(v):
    total = v[:, :128]
    for k in range(1, v.shape[1] // 128):
        total = total + v[:, k * 128 : (k + 1) * 128]
    return total


def layer_kernel(*refs):
    place, counts = refs[:2]
    e_refs = refs[2:10]
    a_refs = refs[10:15]
    b_refs = refs[15:24]
    pick, cot, q_gain, k_gain = refs[24:28]
    att, own_out, other_out, stats_out, ms_out = refs[28:33]
    e, w, normed, acc, grad, grad_v, acc1, acc2, sems = refs[33:]
    x, y, z, c = place[0], place[1], place[2], place[3]

    copies = []

    def go(src, dst):
        copy = pltpu.make_async_copy(src, dst, sems.at[len(copies)])
        copy.start()
        copies.append(copy)

    for k in range(NX):
        xk = lax.rem(x + k, NX)
        go(e_refs[k], e.at[2 * xk + c])
        go(e_refs[NX + k], e.at[2 * xk + 1 - c])
    n_e = len(copies)
    first = pl.ds(0, HW)
    second = pl.ds(HW, HW)
    for k in range(3):
        yk = lax.rem(y + (0, NY - 1, 1)[k], NY)
        go(a_refs[k], w.at[pl.ds(2 * yk, 2), :, first])
    y2 = lax.rem(y + 2, NY)
    go(a_refs[3], w.at[2 * y2, :, first])
    go(a_refs[4], w.at[2 * y2 + 1, :, first])
    for k in range(7):
        zk = lax.rem(z + (0, NZ - 1, 1, NZ - 2, 2, NZ - 3, 3)[k], NZ)
        at = pl.multiple_of(zk * STRIP, STRIP)
        go(b_refs[k], w.at[:, pl.ds(at, STRIP), second])
    z4 = pl.multiple_of(lax.rem(z + 4, NZ) * STRIP, STRIP)
    go(b_refs[7], w.at[pl.ds(0, 4), pl.ds(z4, STRIP), second])
    go(b_refs[8], w.at[pl.ds(4, 4), pl.ds(z4, STRIP), second])

    for copy in copies[:n_e]:
        copy.wait()
    acc1[...] = jnp.zeros_like(acc1)
    acc2[...] = jnp.zeros_like(acc2)

    def sums(b, carry):
        wide = e[b, :ROWS, :].astype(F32)
        acc1[...] += lanes_sum(wide)
        acc2[...] += lanes_sum(wide * wide)
        return carry

    lax.fori_loop(0, 8, sums, 0)
    mean = jnp.sum(acc1[...], axis=1, keepdims=True) * (1.0 / D)
    square = jnp.sum(acc2[...], axis=1, keepdims=True) * (1.0 / D)
    scale = lax.rsqrt(square - mean * mean + EPS)
    lane = lax.broadcasted_iota(jnp.int32, (ROWS, 128), 1)
    ms_out[...] = jnp.where(lane == 0, mean, scale)

    def norm(b, carry):
        wide = e[b, :ROWS, :].astype(F32)
        gain = gain_of(e[b, ROWS:, :])
        normed[b] = ((wide - mean) * scale * gain).astype(BF16)
        return carry

    lax.fori_loop(0, 8, norm, 0)
    values = dot(normed[2 * x], pick[0]) + dot(normed[2 * x + 1], pick[1])
    values = values.astype(BF16)

    for copy in copies[n_e:]:
        copy.wait()
    acc[...] = jnp.zeros_like(acc)

    def project(b, carry):
        acc[...] += dot(normed[b], w[b])
        return carry

    lax.fori_loop(0, 8, project, 0)

    inv_root = HD ** (-0.5)
    span = 2 * MOST
    row = lax.broadcasted_iota(jnp.int32, (span, span), 0)
    col = lax.broadcasted_iota(jnp.int32, (span, span), 1)
    qg, kg = q_gain[...], k_gain[...]
    masks = []
    for g in range(ROWS // span):
        n0, n1 = counts[2 * g], counts[2 * g + 1]
        top_r = jnp.where(row < MOST, n0, n1 + MOST)
        top_c = jnp.where(col < MOST, n0, n1 + MOST)
        same = jnp.where(row < MOST, 0, 1) == jnp.where(col < MOST, 0, 1)
        masks.append(((row < top_r) & (col < top_c) & same, row[:, :1] < top_r[:, :1]))
    for h in range(HC):
        cols = slice(h * HD, (h + 1) * HD)
        kcols = slice(HW + h * HD, HW + (h + 1) * HD)
        q_unit, q_inv = head_norm(acc[:, cols])
        k_unit, k_inv = head_norm(acc[:, kcols])
        q_hat = (q_unit * qg).astype(BF16)
        k_hat = (k_unit * kg).astype(BF16)
        gq, gk = [], []
        for g in range(ROWS // span):
            rows = slice(g * span, (g + 1) * span)
            allowed, live = masks[g]
            q, k, v, go_ = q_hat[rows], k_hat[rows], values[rows, cols], cot[rows, cols]
            scores = dot(q, k, NT) * inv_root
            raised = jnp.where(allowed, jnp.exp(scores), 0.0)
            totals = jnp.sum(raised, axis=1, keepdims=True)
            totals = jnp.where(live, totals, 1.0)
            probs = raised / totals
            low = probs.astype(BF16)
            att[rows, cols] = dot(low, v).astype(BF16)
            g_probs = dot(go_, v, NT)
            grad_v[rows, cols] = dot(low, go_, TN).astype(BF16)
            g_scores = probs * (g_probs - jnp.sum(probs * g_probs, axis=1, keepdims=True))
            g_low = (g_scores * inv_root).astype(BF16)
            gq.append(dot(g_low, k))
            gk.append(dot(g_low, q, TN))
        grad[:, cols] = head_back(jnp.concatenate(gq, axis=0), q_unit, q_inv, qg).astype(BF16)
        grad[:, kcols] = head_back(jnp.concatenate(gk, axis=0), k_unit, k_inv, kg).astype(BF16)

    acc1[...] = jnp.zeros_like(acc1)
    acc2[...] = jnp.zeros_like(acc2)

    def back(k, core, out, with_values):
        b = 2 * lax.rem(x + k, NX) + core
        part = dot(grad[...], w[b], NT)
        if with_values:
            part = part + dot(grad_v[...], pick[core], NT)
        out[k] = part.astype(BF16)
        t = part * gain_of(e[b, ROWS:, :])
        unit = (e[b, :ROWS, :].astype(F32) - mean) * scale
        acc1[...] += lanes_sum(t)
        acc2[...] += lanes_sum(t * unit)

    for out, core in ((other_out, 1 - c), (own_out, c)):
        back(0, core, out, True)

        def step(k, carry, core=core, out=out):
            back(k, core, out, False)
            return carry

        lax.fori_loop(1, NX, step, 0)
    ones = jnp.ones((8, 128), F32)
    for k, part in enumerate((acc1, acc2)):
        stats_out[k * 8 : (k + 1) * 8, :] = lax.dot_general(
            ones, part[...], NT, preferred_element_type=F32, precision=HIGH
        )


def layer(place, counts, blocks, a_pieces, b_pieces, pick, cot, q_gain, k_gain):
    hbm = [pl.BlockSpec(memory_space=pl.ANY)]
    smem = [pl.BlockSpec(memory_space=pltpu.SMEM)]
    flops = 4 * ROWS * D * 2 * HW
    return pl.pallas_call(
        layer_kernel,
        out_shape=(
            jax.ShapeDtypeStruct((ROWS, HW), BF16),
            jax.ShapeDtypeStruct((NX, ROWS, FB), BF16),
            jax.ShapeDtypeStruct((NX, ROWS, FB), BF16),
            jax.ShapeDtypeStruct((16, ROWS), F32),
            jax.ShapeDtypeStruct((ROWS, 128), F32),
        ),
        in_specs=smem * 2 + hbm * 22 + vmem(4),
        out_specs=tuple(vmem(5)),
        scratch_shapes=[
            pltpu.VMEM((8, EROWS, FB), BF16),
            pltpu.VMEM((8, FB, 2 * HW), BF16),
            pltpu.VMEM((8, ROWS, FB), BF16),
            pltpu.VMEM((ROWS, 2 * HW), F32),
            pltpu.VMEM((ROWS, 2 * HW), BF16),
            pltpu.VMEM((ROWS, HW), BF16),
            pltpu.VMEM((ROWS, 128), F32),
            pltpu.VMEM((ROWS, 128), F32),
            pltpu.SemaphoreType.DMA((22,)),
        ],
        compiler_params=pltpu.CompilerParams(vmem_limit_bytes=48 * 2**20),
        cost_estimate=pl.CostEstimate(flops=flops, bytes_accessed=20000000, transcendentals=100000),
        name="layer",
    )(place, counts, *blocks, *a_pieces, *b_pieces, pick, cot, q_gain, k_gain)


def embed_back_kernel(
    place, own, got, r1, r2, r3, e_own, ms, s0, s1, s2, s3, pix, own_out, send_out, full
):
    y = place[1]
    part = own[...].astype(F32)
    for ref in (got, r1, r2, r3):
        part = part + ref[...].astype(F32)
    mean, scale = ms[:, 0:1], ms[:, 1:2]
    gain = gain_of(e_own[ROWS:, :])
    total = s0[...] + s1[...] + s2[...] + s3[...]
    row = lax.broadcasted_iota(jnp.int32, (16, 128), 0)
    columns = []
    for k in range(2):
        chooser = jnp.where(row == 8 * k, 1.0 / D, 0.0).astype(F32)
        columns.append(
            lax.dot_general(total, chooser, TN, preferred_element_type=F32, precision=HIGH)[:, :1]
        )
    t = part * gain
    unit = (e_own[:ROWS, :].astype(F32) - mean) * scale
    grad = (scale * (t - columns[0] - unit * columns[1])).astype(BF16)
    full[...] = dot(grad, pix[...], TN)
    for k in range(NY):
        at = pl.multiple_of(lax.rem(y + k, NY) * YROWS, YROWS)
        piece = full[pl.ds(at, YROWS), :]
        if k == 0:
            own_out[...] = piece
        else:
            send_out[k - 1] = piece.astype(BF16)


def embed_back(place, *args):
    return pl.pallas_call(
        embed_back_kernel,
        out_shape=(
            jax.ShapeDtypeStruct((YROWS, PATCH), F32),
            jax.ShapeDtypeStruct((NY - 1, YROWS, PATCH), BF16),
        ),
        in_specs=[pl.BlockSpec(memory_space=pltpu.SMEM)] + vmem(12),
        out_specs=tuple(vmem(2)),
        scratch_shapes=[pltpu.VMEM((FB, PATCH), F32)],
        compiler_params=pltpu.CompilerParams(vmem_limit_bytes=32 * 2**20),
        cost_estimate=pl.CostEstimate(
            flops=2 * ROWS * FB * PATCH, bytes_accessed=5000000, transcendentals=0
        ),
        name="embed_back",
    )(place, *args)


def per_device(
    pixels,
    patch_counts,
    pack_index,
    embed_weight,
    norm_gain,
    query_weight,
    key_weight,
    query_gain,
    key_gain,
    cotangent,
):
    d = lax.axis_index("dp")
    x = lax.axis_index("mp")
    c = d % NC
    z = (d // NC) % NZ
    y = d // (NC * NZ)
    place = jnp.stack([x, y, z, c]).astype(jnp.int32)

    strip = jnp.swapaxes(embed_weight.reshape(PATCH, PIECE), 0, 1)
    around = [strip] + [z_shift(strip, -k) for k in range(1, NZ)]
    embed_0 = turn(around, NZ - z, 0)
    embed_pieces = [embed_0] + [y_shift(embed_0, -k) for k in range(1, NY)]

    positions = jnp.arange(MOST, dtype=jnp.int32)
    slot_here = (pack_index - d) % NDP
    source = pixels.reshape(IMG_LOAD, MOST, PATCH)
    source = jnp.where(positions[None, :, None] < patch_counts[:, None, None], source, 0)
    facts = jnp.stack([patch_counts, slot_here], axis=1).astype(BF16)
    facts = jnp.broadcast_to(facts[:, None, :], (IMG_LOAD, MOST, 2))
    source = jnp.concatenate([source, facts], axis=2).reshape(IMG_LOAD * MOST, PATCH + 2)
    both = by_core(c, source, core_swap(source), 0)
    pix = both[:, :PATCH]
    facts = both[::MOST, PATCH:].astype(jnp.int32)
    counts, slots = facts[:, 0], facts[:, 1].reshape(NC, IMG_LOAD)

    def half(w, core):
        part = lax.dynamic_slice_in_dim(w, core * HW, HW, axis=1)
        part = part.reshape(2, NC, PIECE, HW).swapaxes(0, 1)
        return part.reshape(NC, 2 * PIECE, HW)

    mine = jnp.stack([half(query_weight, c), half(key_weight, c)])
    send = jnp.stack([half(query_weight, 1 - c), half(key_weight, 1 - c)])
    shard = by_core(c, mine, core_swap(send), 2)
    a0, b0 = shard[0], shard[1]

    al1, ar1 = z_shift(a0, 1), z_shift(a0, -1)
    al2, ar2 = z_shift(al1, 1), z_shift(ar1, -1)
    al3, ar3 = z_shift(al2, 1), z_shift(ar2, -1)
    al4 = z_shift(al3, 1)
    a_own = turn([a0, ar1, ar2, ar3, al4, al3, al2, al1], NZ - z, 1)
    a_low, a_high = y_shift(a_own, 1), y_shift(a_own, -1)
    a_pieces = [a_own, a_low, a_high, y_shift(a_low[0], 1), y_shift(a_high[1], -1)]

    b_own = turn([b0] + [y_shift(b0, -k) for k in range(1, NY)], NY - y, 0)
    bl1, br1 = z_shift(b_own, 1), z_shift(b_own, -1)
    bl2, br2 = z_shift(bl1, 1), z_shift(br1, -1)
    bl3, br3 = z_shift(bl2, 1), z_shift(br2, -1)
    bl4, br4 = z_shift(bl3[:4], 1), z_shift(br3[4:], -1)
    b_pieces = [b_own, bl1, br1, bl2, br2, bl3, br3, bl4, br4]

    gain_here = jnp.where(
        c == 0, norm_gain.reshape(-1, NC, PIECE)[:, 0], norm_gain.reshape(-1, NC, PIECE)[:, 1]
    ).reshape(1, FB)
    e_own = embed(place, pix, embed_pieces, gain_here)
    blocks = [e_own] + [x_shift(e_own, -k) for k in range(1, NX)]
    blocks = blocks + [core_swap(v) for v in blocks]

    cot_mine = lax.dynamic_slice_in_dim(cotangent, c * HW, HW, axis=1)
    cot_send = lax.dynamic_slice_in_dim(cotangent, (1 - c) * HW, HW, axis=1)
    packs = by_core(c, cot_mine[None], core_swap(cot_send)[None], 0)
    packs = packs.reshape(NC, REACH, MOST, HW)
    near = chip_shift(jnp.stack([packs[0, 1], packs[0, 2], packs[1, 2], packs[1, 3]]), -1)
    far = chip_shift(packs[0, 3], -2)
    slot_cot = (
        (packs[0, 0], packs[1, 1], near[1], near[3]),
        (packs[1, 0], near[0], near[2], far),
    )
    cot_rows = []
    for a in range(NC):
        for i in range(IMG_LOAD):
            row = jnp.zeros((MOST, HW), BF16)
            for s in range(REACH):
                row = jnp.where(slots[a, i] == s, slot_cot[a][s], row)
            cot_rows.append(row)
    cot = jnp.concatenate(cot_rows, axis=0)

    column = jnp.arange(HW, dtype=jnp.int32)[None, None, :]
    feature = (c * HC + column // HD) * (D // HEADS) + column % HD
    at = (feature // (NC * PIECE)) * PIECE + feature % PIECE
    part = (feature // PIECE) % NC
    pick = (
        (jnp.arange(FB, dtype=jnp.int32)[None, :, None] == at)
        & (jnp.arange(NC, dtype=jnp.int32)[:, None, None] == part)
    ).astype(BF16)

    att, own_grad, other_grad, stats, ms = layer(
        place,
        counts,
        blocks,
        a_pieces,
        b_pieces,
        pick,
        cot,
        query_gain.reshape(1, HD),
        key_gain.reshape(1, HD),
    )

    got = core_swap(other_grad)
    stats = stats + core_swap(stats)
    pair = [
        (own_grad[k].astype(F32) + got[k].astype(F32)).astype(BF16) for k in range(1, NX)
    ]
    arrived = [x_shift(pair[k - 1], k) for k in range(1, NX)]
    all_stats = [stats] + [x_shift(stats, k) for k in range(1, NX)]
    grad_own, grad_send = embed_back(
        place, own_grad[0], got[0], *arrived, e_own, ms, *all_stats, pix
    )
    total = grad_own
    for k in range(1, NY):
        total = total + y_shift(grad_send[k - 1], k).astype(F32)
    total = total.reshape(NZ, PIECE, PATCH)
    total = lax.dynamic_slice_in_dim(jnp.concatenate([total, total]), z, NZ, axis=0)
    embed_grad = total[0]
    low = total.astype(BF16)
    for k in range(1, NZ):
        embed_grad = embed_grad + z_shift(low[k], k).astype(F32)
    embed_grad = jnp.swapaxes(embed_grad, 0, 1).reshape(PATCH, 1, PIECE)

    shaped = att.reshape(NC, IMG_LOAD, MOST, HW)
    placed = []
    for a in range(NC):
        for s in range(REACH):
            row = jnp.zeros((MOST, HW), BF16)
            for i in range(IMG_LOAD):
                row = jnp.where(slots[a, i] == s, shaped[a, i], row)
            placed.append(row)
    near = chip_shift(jnp.stack([placed[2], placed[3], placed[5], placed[6]]), 1)
    far = chip_shift(placed[7], 2)
    packs = jnp.concatenate(
        [placed[0], near[2], near[0], far, placed[4], placed[1], near[3], near[1]], axis=0
    ).reshape(NC, PACK, HW)
    keep = jnp.where(c == 0, packs[0], packs[1])
    give = jnp.where(c == 0, packs[1], packs[0])
    attended = by_core(c, keep, core_swap(give), 1)
    return attended, embed_grad


def solution(mesh):
    placed = (
        P("dp", None),
        P("dp"),
        P("dp"),
        P(None, "mp", "dp"),
        P("mp"),
        P("dp", "mp"),
        P("dp", "mp"),
        P(),
        P(),
        P("dp", "mp"),
    )
    return jax.shard_map(
        per_device,
        mesh=mesh,
        in_specs=placed,
        out_specs=(P("dp", "mp"), P(None, "mp", "dp")),
        check_vma=False,
    )
```

```python
import functools

import jax
import jax.numpy as jnp
from jax import lax
from jax.experimental import pallas as pl
from jax.experimental.pallas import tpu as pltpu
from jax.sharding import Mesh
from jax.sharding import PartitionSpec as P

D = 6144
HEADS = 24
HD = 128
PATCH = 588
MOST = 48
IMG_LOAD = 3
REACH = 4
EPS = 1e-06

NY, NZ, NC, NX = 4, 8, 2, 4
NDP = NY * NZ * NC
FX = D // NX
FB = FX // NC
HC = HEADS // NX // NC
HW = HC * HD
ROWS = NC * IMG_LOAD * MOST
EROWS = ROWS + 16
STRIP = FB // NZ
PACK = REACH * MOST
PIECE = FX // NDP
YROWS = NZ * PIECE
NT = (((1,), (1,)), ((), ()))
TN = (((0,), (0,)), ((), ()))
F32 = jnp.float32
BF16 = jnp.bfloat16
HIGH = lax.Precision.HIGHEST


def dot(a, b, dims=(((1,), (0,)), ((), ()))):
    return lax.dot_general(a, b, dims, preferred_element_type=F32)


def ring(v, axis, n, k):
    return lax.ppermute(v, axis, [(i, (i + k) % n) for i in range(n)])


def core_swap(v):
    return ring(v, "core", NC, 1)


def z_shift(v, k):
    return ring(v, "z", NZ, k)


def z_swap(v, step):
    return lax.ppermute(v, "z", [(i, i ^ step) for i in range(NZ)])


def y_shift(v, k):
    return ring(v, "y", NY, k)


def x_shift(v, k):
    return ring(v, "x", NX, k)


def chip_shift(v, k):
    return ring(v, ("y", "z"), NY * NZ, k)


def by_core(core, mine, other, axis):
    return jnp.where(
        core == 0,
        jnp.concatenate([mine, other], axis=axis),
        jnp.concatenate([other, mine], axis=axis),
    )


def turn(pieces, start, axis):
    n = len(pieces)
    double = jnp.concatenate(list(pieces) + list(pieces), axis=axis)
    size = pieces[0].shape[axis]
    return lax.dynamic_slice_in_dim(double, start * size, n * size, axis=axis)


def vmem(n):
    return [pl.BlockSpec(memory_space=pltpu.VMEM)] * n


def regroup(rows):
    wide = rows.astype(F32)
    order = [wide[(2 * q + k) * PIECE : (2 * q + k + 1) * PIECE] for k in range(2) for q in range(2)]
    return jnp.concatenate(order, axis=0).astype(BF16)


def prep_kernel(
    place, counts, packs, wq_in, wk_in, cot_in, pix_in, send, kept, source, wq, wk, cot, pix, sems
):
    y, z, c = place[1], place[2], place[3]
    pairs = ((pix_in, pix), (wq_in, wq), (wk_in, wk), (cot_in, cot))
    copies = [pltpu.make_async_copy(a, b, sems.at[k]) for k, (a, b) in enumerate(pairs)]
    for copy in copies:
        copy.start()
    for copy in copies:
        copy.wait()
    d = (y * NZ + z) * NC + c
    lane = lax.broadcasted_iota(jnp.int32, (MOST, 2 * HW), 1)
    row = lax.broadcasted_iota(jnp.int32, (MOST, 2 * HW), 0)
    source[...] = jnp.zeros_like(source)
    source[:, :PATCH] = pix[...]
    for i in range(IMG_LOAD):
        rows = pl.ds(i * MOST, MOST)
        n = counts[i]
        slot = lax.rem(packs[i] - d + NDP, NDP)
        values = jnp.where(row < n, source[rows, :].astype(F32), 0.0)
        values = jnp.where(lane == PATCH, n.astype(F32), values)
        values = jnp.where(lane == PATCH + 1, slot.astype(F32), values)
        source[rows, :] = values.astype(BF16)

    n_w = 2 * NC * PIECE
    halves = (slice(0, HW), slice(HW, 2 * HW))
    for core in range(NC):

        @pl.when(c == core)
        def _(core=core):
            for k, w in enumerate((wq, wk)):
                kept[k * n_w : (k + 1) * n_w, :] = regroup(w[:, halves[core]])
                send[k * n_w : (k + 1) * n_w, :] = regroup(w[:, halves[1 - core]])
            kept[2 * n_w :, :] = cot[:, halves[core]]
            send[2 * n_w : 2 * n_w + PACK, :] = cot[:, halves[1 - core]]

    at = 2 * n_w + PACK
    for k in range(2):
        send[at + k * IMG_LOAD * MOST : at + (k + 1) * IMG_LOAD * MOST, :] = source[:, halves[k]]


def prep(place, counts, packs, wq, wk, cot, pix):
    n_w = 2 * NC * PIECE
    return pl.pallas_call(
        prep_kernel,
        out_shape=(
            jax.ShapeDtypeStruct((2 * n_w + PACK + 2 * IMG_LOAD * MOST, HW), BF16),
            jax.ShapeDtypeStruct((2 * n_w + PACK, HW), BF16),
            jax.ShapeDtypeStruct((IMG_LOAD * MOST, 2 * HW), BF16),
        ),
        in_specs=[pl.BlockSpec(memory_space=pltpu.SMEM)] * 3
        + [pl.BlockSpec(memory_space=pltpu.HBM)] * 4,
        out_specs=tuple(vmem(3)),
        scratch_shapes=[
            pltpu.VMEM(wq.shape, BF16),
            pltpu.VMEM(wk.shape, BF16),
            pltpu.VMEM(cot.shape, BF16),
            pltpu.VMEM(pix.shape, BF16),
            pltpu.SemaphoreType.DMA((4,)),
        ],
        compiler_params=pltpu.CompilerParams(vmem_limit_bytes=60 * 2**20),
        cost_estimate=pl.CostEstimate(flops=1000000, bytes_accessed=2000000, transcendentals=0),
        name="prep",
    )(place, counts, packs, wq, wk, cot, pix)


def order_kernel(place, *refs):
    pieces, out = refs[:-1], refs[-1]
    for k, piece in enumerate(pieces):
        out[pl.ds(2 * lax.rem(place[1] + k, NY), 2)] = piece[...]


def in_order(place, pieces):
    return pl.pallas_call(
        order_kernel,
        out_shape=jax.ShapeDtypeStruct((NY * NC, STRIP, HW), BF16),
        in_specs=[pl.BlockSpec(memory_space=pltpu.SMEM)] + vmem(len(pieces)),
        out_specs=pl.BlockSpec(memory_space=pltpu.VMEM),
        cost_estimate=pl.CostEstimate(flops=0, bytes_accessed=2000000, transcendentals=0),
        name="order",
    )(place, *pieces)


def embed_kernel(place, source, got, w0, w1, w2, w3, gain, out, pix, facts, weights):
    y, c = place[1], place[3]
    for k, piece in enumerate((w0, w1, w2, w3)):
        at = pl.multiple_of(lax.rem(y + k, NY) * YROWS, YROWS)
        weights[pl.ds(at, YROWS), :] = piece[...]
    half = IMG_LOAD * MOST
    at = 4 * NC * PIECE + PACK
    mine = source[...]
    other = jnp.concatenate([got[at : at + half, :], got[at + half : at + 2 * half, :]], axis=1)
    low = jnp.where(c == 0, mine, other)
    high = jnp.where(c == 0, other, mine)
    pix[:half, :] = low[:, :PATCH]
    pix[half:, :] = high[:, :PATCH]
    first = PATCH // 128 * 128
    for core, part in enumerate((low, high)):
        wide = part[:, first : first + 128].astype(F32)
        for i in range(IMG_LOAD):
            k = core * IMG_LOAD + i
            facts[k : k + 1, :] = wide[i * MOST : i * MOST + 1, :].astype(jnp.int32)
    facts[NC * IMG_LOAD :, :] = jnp.zeros((8 - NC * IMG_LOAD, 128), jnp.int32)
    out[:ROWS, :] = dot(pix[...], weights[...], NT).astype(BF16)
    full = gain[...]
    high = full.astype(BF16)
    rest = full - high.astype(F32)
    mid = rest.astype(BF16)
    low = (rest - mid.astype(F32)).astype(BF16)
    row = lax.broadcasted_iota(jnp.int32, (16, FB), 0)
    out[ROWS:, :] = jnp.where(
        row == 0,
        high.astype(F32),
        jnp.where(row == 1, mid.astype(F32), jnp.where(row == 2, low.astype(F32), 0.0)),
    ).astype(BF16)


def embed(place, source, got, pieces, gain):
    return pl.pallas_call(
        embed_kernel,
        out_shape=(
            jax.ShapeDtypeStruct((EROWS, FB), BF16),
            jax.ShapeDtypeStruct((ROWS, PATCH), BF16),
            jax.ShapeDtypeStruct((8, 128), jnp.int32),
        ),
        in_specs=[pl.BlockSpec(memory_space=pltpu.SMEM)] + vmem(7),
        out_specs=tuple(vmem(3)),
        scratch_shapes=[pltpu.VMEM((FB, PATCH), BF16)],
        compiler_params=pltpu.CompilerParams(vmem_limit_bytes=24 * 2**20),
        cost_estimate=pl.CostEstimate(
            flops=2 * ROWS * FB * PATCH, bytes_accessed=2000000, transcendentals=0
        ),
        name="embed",
    )(place, source, got, *pieces, gain)


def gain_of(rows):
    wide = rows.astype(F32)
    return wide[0:1] + wide[1:2] + wide[2:3]


def head_norm(values):
    center = jnp.mean(values, axis=1, keepdims=True)
    spread = jnp.mean(values * values, axis=1, keepdims=True) - center * center
    inv = lax.rsqrt(spread + EPS)
    return (values - center) * inv, inv


def head_back(grad_hat, unit, inv, gain):
    t = grad_hat * gain
    mean_t = jnp.mean(t, axis=1, keepdims=True)
    second = jnp.mean(t * unit, axis=1, keepdims=True)
    return inv * (t - mean_t - unit * second)


def lanes_sum(v):
    total = v[:, :128]
    for k in range(1, v.shape[1] // 128):
        total = total + v[:, k * 128 : (k + 1) * 128]
    return total


def norm_kernel(place, e, pick, normed, values, ms_out, acc1, acc2):
    x = place[0]
    acc1[...] = jnp.zeros_like(acc1)
    acc2[...] = jnp.zeros_like(acc2)

    def sums(b, carry):
        wide = e[b, :ROWS, :].astype(F32)
        acc1[...] += lanes_sum(wide)
        acc2[...] += lanes_sum(wide * wide)
        return carry

    lax.fori_loop(0, 8, sums, 0)
    mean = jnp.sum(acc1[...], axis=1, keepdims=True) * (1.0 / D)
    square = jnp.sum(acc2[...], axis=1, keepdims=True) * (1.0 / D)
    scale = lax.rsqrt(square - mean * mean + EPS)
    lane = lax.broadcasted_iota(jnp.int32, (ROWS, 128), 1)
    ms_out[...] = jnp.where(lane == 0, mean, scale)

    def norm(b, carry):
        wide = e[b, :ROWS, :].astype(F32)
        gain = gain_of(e[b, ROWS:, :])
        normed[b] = ((wide - mean) * scale * gain).astype(BF16)
        return carry

    lax.fori_loop(0, 8, norm, 0)
    picked = dot(normed[2 * x], pick[0]) + dot(normed[2 * x + 1], pick[1])
    values[...] = picked.astype(BF16)


def norm_rows(place, blocks, pick):
    return pl.pallas_call(
        norm_kernel,
        out_shape=(
            jax.ShapeDtypeStruct((8, ROWS, FB), BF16),
            jax.ShapeDtypeStruct((ROWS, HW), BF16),
            jax.ShapeDtypeStruct((ROWS, 128), F32),
        ),
        in_specs=[pl.BlockSpec(memory_space=pltpu.SMEM)] + vmem(2),
        out_specs=tuple(vmem(3)),
        scratch_shapes=[pltpu.VMEM((ROWS, 128), F32), pltpu.VMEM((ROWS, 128), F32)],
        compiler_params=pltpu.CompilerParams(vmem_limit_bytes=24 * 2**20),
        cost_estimate=pl.CostEstimate(
            flops=4 * ROWS * FB * HW, bytes_accessed=12000000, transcendentals=0
        ),
        name="norm",
    )(place, blocks, pick)


def layer_kernel(*refs):
    place, facts, e, normed, values, ms = refs[:6]
    a_refs, b_refs = refs[6:11], refs[11:20]
    pick, packs, near, far, q_gain, k_gain = refs[20:26]
    att_here, att_near, att_far, own_out, other_out = refs[26:31]
    w, acc, grad, grad_v, acc1, acc2, cot, att, sems = refs[31:]
    x, y, z, c = place[0], place[1], place[2], place[3]
    first = pl.ds(0, HW)
    second = pl.ds(HW, HW)
    copies = []

    def go(src, dst):
        copies.append(pltpu.make_async_copy(src, dst, sems.at[len(copies)]))
        copies[-1].start()

    for core in range(NC):
        for k in range(3):
            yk = lax.rem(y + (0, NY - 1, 1)[k], NY)
            go(a_refs[k].at[:, core], w.at[2 * yk + core, :, :, first])
        for k in range(2):
            yk = lax.rem(y + 2, NY)
            go(a_refs[3 + k].at[:, core], w.at[2 * yk + core, pl.ds(4 * k, 4), :, first])
    for k in range(9):
        zk = lax.rem(z + (0, NZ - 1, 1, NZ - 2, 2, NZ - 3, 3, 4, 4)[k], NZ)
        rows = pl.ds(0, 8) if k < 7 else pl.ds(4 * (k - 7), 4)
        go(b_refs[k], w.at[rows, zk, :, second])
    acc[...] = jnp.zeros_like(acc)
    n_at = PATCH % 128
    counts = [facts[i, n_at] for i in range(NC * IMG_LOAD)]
    slots = [facts[i, n_at + 1] for i in range(NC * IMG_LOAD)]
    by_slot = (
        (packs[0, 0], packs[1, 1], near[1], near[3]),
        (packs[1, 0], near[0], near[2], far[...]),
    )
    for i, slot in enumerate(slots):
        rows = jnp.zeros((MOST, HW), F32)
        for k in range(REACH):
            piece = by_slot[i // IMG_LOAD][k].astype(F32)
            rows = jnp.where(slot == k, piece, rows)
        cot[i * MOST : (i + 1) * MOST, :] = rows.astype(BF16)
    for copy in copies:
        copy.wait()

    def block(b):
        return w[b].reshape(FB, 2 * HW)

    def project(b, carry):
        acc[...] += dot(normed[b], block(b))
        return carry

    lax.fori_loop(0, 8, project, 0)

    inv_root = HD ** (-0.5)
    span = 2 * MOST
    row = lax.broadcasted_iota(jnp.int32, (span, span), 0)
    col = lax.broadcasted_iota(jnp.int32, (span, span), 1)
    qg, kg = q_gain[...], k_gain[...]
    masks = []
    for g in range(ROWS // span):
        n0, n1 = counts[2 * g], counts[2 * g + 1]
        top_r = jnp.where(row < MOST, n0, n1 + MOST)
        top_c = jnp.where(col < MOST, n0, n1 + MOST)
        same = jnp.where(row < MOST, 0, 1) == jnp.where(col < MOST, 0, 1)
        masks.append(((row < top_r) & (col < top_c) & same, row[:, :1] < top_r[:, :1]))
    for h in range(HC):
        cols = slice(h * HD, (h + 1) * HD)
        kcols = slice(HW + h * HD, HW + (h + 1) * HD)
        q_unit, q_inv = head_norm(acc[:, cols])
        k_unit, k_inv = head_norm(acc[:, kcols])
        q_hat = (q_unit * qg).astype(BF16)
        k_hat = (k_unit * kg).astype(BF16)
        gq, gk = [], []
        for g in range(ROWS // span):
            rows = slice(g * span, (g + 1) * span)
            allowed, live = masks[g]
            q, k, v, go = q_hat[rows], k_hat[rows], values[rows, cols], cot[rows, cols]
            scores = dot(q, k, NT) * inv_root
            raised = jnp.where(allowed, jnp.exp(scores), 0.0)
            totals = jnp.sum(raised, axis=1, keepdims=True)
            totals = jnp.where(live, totals, 1.0)
            probs = raised / totals
            low = probs.astype(BF16)
            att[rows, cols] = dot(low, v).astype(BF16)
            g_probs = dot(go, v, NT)
            grad_v[rows, cols] = dot(low, go, TN).astype(BF16)
            g_scores = probs * (g_probs - jnp.sum(probs * g_probs, axis=1, keepdims=True))
            g_low = (g_scores * inv_root).astype(BF16)
            gq.append(dot(g_low, k))
            gk.append(dot(g_low, q, TN))
        grad[:, cols] = head_back(jnp.concatenate(gq, axis=0), q_unit, q_inv, qg).astype(BF16)
        grad[:, kcols] = head_back(jnp.concatenate(gk, axis=0), k_unit, k_inv, kg).astype(BF16)

    goes = (
        ((att_here, 0), (att_here, 1), (att_near, 0), (att_near, 1)),
        ((att_here, 2), (att_near, 2), (att_near, 3), (att_far, 0)),
    )
    for core in range(NC):
        for k, (out, at) in enumerate(goes[core]):
            rows = jnp.zeros((MOST, HW), F32)
            for i in range(core * IMG_LOAD, (core + 1) * IMG_LOAD):
                piece = att[i * MOST : (i + 1) * MOST, :].astype(F32)
                rows = jnp.where(slots[i] == k, piece, rows)
            out[at] = rows.astype(BF16)

    acc1[...] = jnp.zeros_like(acc1)
    acc2[...] = jnp.zeros_like(acc2)
    mean, scale = ms[:, 0:1], ms[:, 1:2]

    def back(k, core, out, with_values):
        b = 2 * lax.rem(x + k, NX) + core
        part = dot(grad[...], block(b), NT)
        if with_values:
            part = part + dot(grad_v[...], pick[core], NT)
        out[k, :ROWS, :] = part.astype(BF16)
        t = part * gain_of(e[b, ROWS:, :])
        unit = (e[b, :ROWS, :].astype(F32) - mean) * scale
        acc1[...] += lanes_sum(t)
        acc2[...] += lanes_sum(t * unit)

    for out, core in ((other_out, 1 - c), (own_out, c)):
        back(0, core, out, True)

        def step(k, carry, core=core, out=out):
            back(k, core, out, False)
            return carry

        lax.fori_loop(1, NX, step, 0)
    ones = jnp.ones((8, 128), F32)
    stats = []
    for part in (acc1, acc2):
        total = lax.dot_general(ones, part[...], NT, preferred_element_type=F32, precision=HIGH)
        stats.append(jnp.concatenate([total, jnp.zeros((8, FB - ROWS), F32)], axis=1))
    rows = stat_rows(stats[0][:1], stats[1][:1])
    for out in (own_out, other_out):
        for k in range(NX):
            out[k, ROWS:, :] = rows


def stat_rows(first, second):
    row = lax.broadcasted_iota(jnp.int32, (16, FB), 0)
    parts = []
    for v in (first, second):
        high = v.astype(BF16).astype(F32)
        parts += [high, v - high]
    out = jnp.zeros((16, FB), F32)
    for k in range(4):
        out = jnp.where(row == k, parts[k], out)
    return out.astype(BF16)


def stats_of(rows):
    wide = rows.astype(F32)
    return wide[0:1] + wide[1:2], wide[2:3] + wide[3:4]


def layer(place, facts, rows, a_pieces, b_pieces, pick, cot_pieces, q_gain, k_gain):
    hbm = [pl.BlockSpec(memory_space=pltpu.HBM)]
    smem = [pl.BlockSpec(memory_space=pltpu.SMEM)]
    flops = 4 * ROWS * D * 2 * HW
    return pl.pallas_call(
        layer_kernel,
        out_shape=(
            jax.ShapeDtypeStruct((3, MOST, HW), BF16),
            jax.ShapeDtypeStruct((4, MOST, HW), BF16),
            jax.ShapeDtypeStruct((1, MOST, HW), BF16),
            jax.ShapeDtypeStruct((NX, EROWS, FB), BF16),
            jax.ShapeDtypeStruct((NX, EROWS, FB), BF16),
        ),
        in_specs=smem * 2 + vmem(4) + hbm * 14 + vmem(6),
        out_specs=tuple(vmem(5)),
        scratch_shapes=[
            pltpu.VMEM((8, NZ, STRIP, 2 * HW), BF16),
            pltpu.VMEM((ROWS, 2 * HW), F32),
            pltpu.VMEM((ROWS, 2 * HW), BF16),
            pltpu.VMEM((ROWS, HW), BF16),
            pltpu.VMEM((ROWS, 128), F32),
            pltpu.VMEM((ROWS, 128), F32),
            pltpu.VMEM((ROWS, HW), BF16),
            pltpu.VMEM((ROWS, HW), BF16),
            pltpu.SemaphoreType.DMA((19,)),
        ],
        compiler_params=pltpu.CompilerParams(vmem_limit_bytes=40 * 2**20),
        cost_estimate=pl.CostEstimate(flops=flops, bytes_accessed=20000000, transcendentals=100000),
        name="layer",
    )(place, facts, *rows, *a_pieces, *b_pieces, pick, *cot_pieces, q_gain, k_gain)


def pair_kernel(own, got, *outs):
    for k, out in enumerate(outs):
        out[:ROWS, :] = (own[k, :ROWS, :].astype(F32) + got[k, :ROWS, :].astype(F32)).astype(BF16)
        a, b = stats_of(own[k, ROWS:, :]), stats_of(got[k, ROWS:, :])
        out[ROWS:, :] = stat_rows(a[0] + b[0], a[1] + b[1])


def pair_sum(own, got):
    return pl.pallas_call(
        pair_kernel,
        out_shape=(jax.ShapeDtypeStruct((EROWS, FB), BF16),) * NX,
        in_specs=vmem(2),
        out_specs=tuple(vmem(NX)),
        compiler_params=pltpu.CompilerParams(vmem_limit_bytes=16 * 2**20),
        cost_estimate=pl.CostEstimate(flops=1000000, bytes_accessed=6000000, transcendentals=0),
        name="pair_sum",
    )(own, got)


def embed_back_kernel(
    place, own, r1, r2, r3, e_own, ms, pix, own_out, send_out, full
):
    y = place[1]
    part = own[:ROWS, :].astype(F32)
    sums = stats_of(own[ROWS:, :])
    for ref in (r1, r2, r3):
        part = part + ref[:ROWS, :].astype(F32)
        more = stats_of(ref[ROWS:, :])
        sums = (sums[0] + more[0], sums[1] + more[1])
    mean, scale = ms[:, 0:1], ms[:, 1:2]
    gain = gain_of(e_own[ROWS:, :])
    chooser = jnp.where(lax.broadcasted_iota(jnp.int32, (8, 128), 0) == 0, 1.0 / D, 0.0)
    columns = []
    for v in sums:
        tall = jnp.broadcast_to(v[:, :ROWS], (8, ROWS))
        columns.append(
            lax.dot_general(tall, chooser, TN, preferred_element_type=F32, precision=HIGH)[:, :1]
        )
    t = part * gain
    unit = (e_own[:ROWS, :].astype(F32) - mean) * scale
    grad = (scale * (t - columns[0] - unit * columns[1])).astype(BF16)
    full[...] = dot(grad, pix[...], TN)
    for k in range(NY):
        at = pl.multiple_of(lax.rem(y + k, NY) * YROWS, YROWS)
        piece = full[pl.ds(at, YROWS), :]
        if k == 0:
            own_out[...] = piece
        else:
            send_out[k - 1] = piece.astype(BF16)


def embed_back(place, *args):
    return pl.pallas_call(
        embed_back_kernel,
        out_shape=(
            jax.ShapeDtypeStruct((YROWS, PATCH), F32),
            jax.ShapeDtypeStruct((NY - 1, YROWS, PATCH), BF16),
        ),
        in_specs=[pl.BlockSpec(memory_space=pltpu.SMEM)] + vmem(7),
        out_specs=tuple(vmem(2)),
        scratch_shapes=[pltpu.VMEM((FB, PATCH), F32)],
        compiler_params=pltpu.CompilerParams(vmem_limit_bytes=32 * 2**20),
        cost_estimate=pl.CostEstimate(
            flops=2 * ROWS * FB * PATCH, bytes_accessed=5000000, transcendentals=0
        ),
        name="embed_back",
    )(place, *args)


def per_device(
    pixels,
    patch_counts,
    pack_index,
    embed_weight,
    norm_gain,
    query_weight,
    key_weight,
    query_gain,
    key_gain,
    cotangent,
):
    x, y, z, c = [lax.axis_index(name) for name in ("x", "y", "z", "core")]
    d = (y * NZ + z) * NC + c
    place = jnp.stack([x, y, z, c]).astype(jnp.int32)

    strip = jnp.swapaxes(embed_weight.reshape(PATCH, PIECE), 0, 1)
    strip = by_core(z % 2, strip, z_swap(strip, 1), 0)
    sent, kept, source = prep(
        place, patch_counts, pack_index, query_weight, key_weight, cotangent, pixels
    )
    got = core_swap(sent)
    n_w = 2 * NC * PIECE
    shards = []
    for k in range(2):
        rows = slice(k * n_w, (k + 1) * n_w)
        mine = kept[rows].reshape(NC, 2 * PIECE, HW)
        shards.append(by_core(c, mine, got[rows].reshape(NC, 2 * PIECE, HW), 1))
    a0, b0 = shards

    after = lax.optimization_barrier
    a_own = lax.all_gather(a0, "z", axis=0, tiled=False)
    b_near = [y_shift(b0, -k) for k in range(1, NY)]
    for step in (2, 4):
        strip = by_core(z // step % 2, strip, z_swap(strip, step), 0)
    strip, b_near = after((strip, b_near))
    b_own = in_order(place, [b0] + b_near)
    embed_pieces = [strip] + [y_shift(strip, -k) for k in range(1, NY)]
    bl1, br1 = z_shift(b_own, 1), z_shift(b_own, -1)
    bl2, br2 = z_shift(bl1, 1), z_shift(br1, -1)
    bl3, br3 = z_shift(bl2, 1), z_shift(br2, -1)
    bl4, br4 = z_shift(bl3[:4], 1), z_shift(br3[4:], -1)
    a_low, a_high = y_shift(a_own, 1), y_shift(a_own, -1)
    a_pieces = [a_own, a_low, a_high, y_shift(a_low[:4], 1), y_shift(a_high[4:], -1)]
    b_pieces = [b_own, bl1, br1, bl2, br2, bl3, br3, bl4, br4]

    gain_here = jnp.where(
        c == 0, norm_gain.reshape(-1, NC, PIECE)[:, 0], norm_gain.reshape(-1, NC, PIECE)[:, 1]
    ).reshape(1, FB)
    e_own, pix, facts = embed(place, source, got, embed_pieces, gain_here)
    blocks = lax.all_gather(e_own, ("x", "core"), axis=0, tiled=False)

    kept_cot, got_cot, bl2 = after((kept[2 * n_w :], got[2 * n_w : 2 * n_w + PACK], bl2))
    packs = by_core(c, kept_cot[None], got_cot[None], 0)
    packs = packs.reshape(NC, REACH, MOST, HW)
    near = chip_shift(jnp.stack([packs[0, 1], packs[0, 2], packs[1, 2], packs[1, 3]]), -1)
    far = chip_shift(packs[0, 3], -2)

    column = jnp.arange(HW, dtype=jnp.int32)[None, None, :]
    feature = (c * HC + column // HD) * (D // HEADS) + column % HD
    at = (feature // (NC * PIECE)) * PIECE + feature % PIECE
    part = (feature // PIECE) % NC
    pick = (
        (jnp.arange(FB, dtype=jnp.int32)[None, :, None] == at)
        & (jnp.arange(NC, dtype=jnp.int32)[:, None, None] == part)
    ).astype(BF16)

    normed, values, ms = norm_rows(place, blocks, pick)
    att_here, att_near, att_far, own_grad, other_grad = layer(
        place,
        facts,
        (blocks, normed, values, ms),
        a_pieces,
        b_pieces,
        pick,
        (packs, near, far),
        query_gain.reshape(1, HD),
        key_gain.reshape(1, HD),
    )

    pair = pair_sum(own_grad, core_swap(other_grad))
    arrived = [x_shift(pair[k], k) for k in range(1, NX)]
    grad_own, grad_send = embed_back(place, pair[0], *arrived, e_own, ms, pix)
    total = grad_own
    for k in range(1, NY):
        total = total + y_shift(grad_send[k - 1], k).astype(F32)
    total = total.reshape(NZ, PIECE, PATCH)
    total = lax.dynamic_slice_in_dim(jnp.concatenate([total, total]), z, NZ, axis=0)
    embed_grad = total[0]
    low = total.astype(BF16)
    for k in range(1, NZ):
        embed_grad = embed_grad + z_shift(low[k], k).astype(F32)
    embed_grad = jnp.swapaxes(embed_grad, 0, 1).reshape(PATCH, 1, PIECE)

    near = chip_shift(att_near, 1)
    far = chip_shift(att_far, 2)
    packs = jnp.concatenate(
        [att_here[0], near[2], near[0], far[0], att_here[2], att_here[1], near[3], near[1]], axis=0
    ).reshape(NC, PACK, HW)
    keep = jnp.where(c == 0, packs[0], packs[1])
    give = jnp.where(c == 0, packs[1], packs[0])
    attended = by_core(c, keep, core_swap(give), 1)
    return attended, embed_grad


def solution(mesh):
    chips = Mesh(mesh.devices.reshape(NY, NZ, NC, NX), ("y", "z", "core", "x"))
    dp = ("y", "z", "core")
    placed = (
        P(dp, None),
        P(dp),
        P(dp),
        P(None, "x", dp),
        P("x"),
        P(dp, "x"),
        P(dp, "x"),
        P(),
        P(),
        P(dp, "x"),
    )
    return jax.shard_map(
        per_device,
        mesh=chips,
        in_specs=placed,
        out_specs=(P(dp, "x"), P(None, "x", dp)),
        check_vma=False,
    )
```

```python
import functools

import jax
import jax.numpy as jnp
from jax import lax
from jax.experimental import pallas as pl
from jax.experimental.pallas import tpu as pltpu
from jax.sharding import Mesh
from jax.sharding import PartitionSpec as P

D = 6144
HEADS = 24
HD = 128
PATCH = 588
MOST = 48
IMG_LOAD = 3
REACH = 4
EPS = 1e-06

NY, NZ, NC, NX = 4, 8, 2, 4
NDP = NY * NZ * NC
FX = D // NX
FB = FX // NC
HC = HEADS // NX // NC
HW = HC * HD
ROWS = NC * IMG_LOAD * MOST
EROWS = ROWS + 16
STRIP = FB // NZ
PACK = REACH * MOST
PIECE = FX // NDP
YROWS = NZ * PIECE
NT = (((1,), (1,)), ((), ()))
TN = (((0,), (0,)), ((), ()))
F32 = jnp.float32
BF16 = jnp.bfloat16
HIGH = lax.Precision.HIGHEST


def dot(a, b, dims=(((1,), (0,)), ((), ()))):
    return lax.dot_general(a, b, dims, preferred_element_type=F32)


def ring(v, axis, n, k):
    return lax.ppermute(v, axis, [(i, (i + k) % n) for i in range(n)])


def core_swap(v):
    return ring(v, "core", NC, 1)


def z_shift(v, k):
    return ring(v, "z", NZ, k)


def z_swap(v, step):
    return lax.ppermute(v, "z", [(i, i ^ step) for i in range(NZ)])


def y_shift(v, k):
    return ring(v, "y", NY, k)


def x_shift(v, k):
    return ring(v, "x", NX, k)


def chip_shift(v, k):
    return ring(v, ("y", "z"), NY * NZ, k)


def by_core(core, mine, other, axis):
    return jnp.where(
        core == 0,
        jnp.concatenate([mine, other], axis=axis),
        jnp.concatenate([other, mine], axis=axis),
    )


def turn(pieces, start, axis):
    n = len(pieces)
    double = jnp.concatenate(list(pieces) + list(pieces), axis=axis)
    size = pieces[0].shape[axis]
    return lax.dynamic_slice_in_dim(double, start * size, n * size, axis=axis)


def vmem(n):
    return [pl.BlockSpec(memory_space=pltpu.VMEM)] * n


def regroup(rows):
    wide = rows.astype(F32)
    order = [wide[(2 * q + k) * PIECE : (2 * q + k + 1) * PIECE] for k in range(2) for q in range(2)]
    return jnp.concatenate(order, axis=0).astype(BF16)


def prep_kernel(
    place, counts, packs, wq_in, wk_in, cot_in, pix_in, send, kept, source, wq, wk, cot, pix, sems
):
    y, z, c = place[1], place[2], place[3]
    pairs = ((pix_in, pix), (wq_in, wq), (wk_in, wk), (cot_in, cot))
    copies = [pltpu.make_async_copy(a, b, sems.at[k]) for k, (a, b) in enumerate(pairs)]
    for copy in copies:
        copy.start()
    for copy in copies:
        copy.wait()
    d = (y * NZ + z) * NC + c
    lane = lax.broadcasted_iota(jnp.int32, (MOST, 2 * HW), 1)
    row = lax.broadcasted_iota(jnp.int32, (MOST, 2 * HW), 0)
    source[...] = jnp.zeros_like(source)
    source[:, :PATCH] = pix[...]
    for i in range(IMG_LOAD):
        rows = pl.ds(i * MOST, MOST)
        n = counts[i]
        slot = lax.rem(packs[i] - d + NDP, NDP)
        values = jnp.where(row < n, source[rows, :].astype(F32), 0.0)
        values = jnp.where(lane == PATCH, n.astype(F32), values)
        values = jnp.where(lane == PATCH + 1, slot.astype(F32), values)
        source[rows, :] = values.astype(BF16)

    n_w = 2 * NC * PIECE
    halves = (slice(0, HW), slice(HW, 2 * HW))
    for core in range(NC):

        @pl.when(c == core)
        def _(core=core):
            for k, w in enumerate((wq, wk)):
                kept[k * n_w : (k + 1) * n_w, :] = regroup(w[:, halves[core]])
                send[k * n_w : (k + 1) * n_w, :] = regroup(w[:, halves[1 - core]])
            kept[2 * n_w :, :] = cot[:, halves[core]]
            send[2 * n_w : 2 * n_w + PACK, :] = cot[:, halves[1 - core]]

    at = 2 * n_w + PACK
    for k in range(2):
        send[at + k * IMG_LOAD * MOST : at + (k + 1) * IMG_LOAD * MOST, :] = source[:, halves[k]]


def prep(place, counts, packs, wq, wk, cot, pix):
    n_w = 2 * NC * PIECE
    return pl.pallas_call(
        prep_kernel,
        out_shape=(
            jax.ShapeDtypeStruct((2 * n_w + PACK + 2 * IMG_LOAD * MOST, HW), BF16),
            jax.ShapeDtypeStruct((2 * n_w + PACK, HW), BF16),
            jax.ShapeDtypeStruct((IMG_LOAD * MOST, 2 * HW), BF16),
        ),
        in_specs=[pl.BlockSpec(memory_space=pltpu.SMEM)] * 3
        + [pl.BlockSpec(memory_space=pltpu.HBM)] * 4,
        out_specs=tuple(vmem(3)),
        scratch_shapes=[
            pltpu.VMEM(wq.shape, BF16),
            pltpu.VMEM(wk.shape, BF16),
            pltpu.VMEM(cot.shape, BF16),
            pltpu.VMEM(pix.shape, BF16),
            pltpu.SemaphoreType.DMA((4,)),
        ],
        compiler_params=pltpu.CompilerParams(vmem_limit_bytes=60 * 2**20),
        cost_estimate=pl.CostEstimate(flops=1000000, bytes_accessed=2000000, transcendentals=0),
        name="prep",
    )(place, counts, packs, wq, wk, cot, pix)


def order_kernel(place, *refs):
    pieces, out = refs[:-1], refs[-1]
    for k, piece in enumerate(pieces):
        out[pl.ds(2 * lax.rem(place[1] + k, NY), 2)] = piece[...]


def in_order(place, pieces):
    return pl.pallas_call(
        order_kernel,
        out_shape=jax.ShapeDtypeStruct((NY * NC, STRIP, HW), BF16),
        in_specs=[pl.BlockSpec(memory_space=pltpu.SMEM)] + vmem(len(pieces)),
        out_specs=pl.BlockSpec(memory_space=pltpu.VMEM),
        cost_estimate=pl.CostEstimate(flops=0, bytes_accessed=2000000, transcendentals=0),
        name="order",
    )(place, *pieces)


def embed_kernel(place, source, got, w0, w1, w2, w3, gain, out, pix, facts, weights):
    y, c = place[1], place[3]
    for k, piece in enumerate((w0, w1, w2, w3)):
        at = pl.multiple_of(lax.rem(y + k, NY) * YROWS, YROWS)
        weights[pl.ds(at, YROWS), :] = piece[...]
    half = IMG_LOAD * MOST
    at = 4 * NC * PIECE + PACK
    mine = source[...]
    other = jnp.concatenate([got[at : at + half, :], got[at + half : at + 2 * half, :]], axis=1)
    low = jnp.where(c == 0, mine, other)
    high = jnp.where(c == 0, other, mine)
    pix[:half, :] = low[:, :PATCH]
    pix[half:, :] = high[:, :PATCH]
    first = PATCH // 128 * 128
    for core, part in enumerate((low, high)):
        wide = part[:, first : first + 128].astype(F32)
        for i in range(IMG_LOAD):
            k = core * IMG_LOAD + i
            facts[k : k + 1, :] = wide[i * MOST : i * MOST + 1, :].astype(jnp.int32)
    facts[NC * IMG_LOAD :, :] = jnp.zeros((8 - NC * IMG_LOAD, 128), jnp.int32)
    out[:ROWS, :] = dot(pix[...], weights[...], NT).astype(BF16)
    full = gain[...]
    high = full.astype(BF16)
    rest = full - high.astype(F32)
    mid = rest.astype(BF16)
    low = (rest - mid.astype(F32)).astype(BF16)
    row = lax.broadcasted_iota(jnp.int32, (16, FB), 0)
    out[ROWS:, :] = jnp.where(
        row == 0,
        high.astype(F32),
        jnp.where(row == 1, mid.astype(F32), jnp.where(row == 2, low.astype(F32), 0.0)),
    ).astype(BF16)


def embed(place, source, got, pieces, gain):
    return pl.pallas_call(
        embed_kernel,
        out_shape=(
            jax.ShapeDtypeStruct((EROWS, FB), BF16),
            jax.ShapeDtypeStruct((ROWS, PATCH), BF16),
            jax.ShapeDtypeStruct((8, 128), jnp.int32),
        ),
        in_specs=[pl.BlockSpec(memory_space=pltpu.SMEM)] + vmem(7),
        out_specs=tuple(vmem(3)),
        scratch_shapes=[pltpu.VMEM((FB, PATCH), BF16)],
        compiler_params=pltpu.CompilerParams(vmem_limit_bytes=24 * 2**20),
        cost_estimate=pl.CostEstimate(
            flops=2 * ROWS * FB * PATCH, bytes_accessed=2000000, transcendentals=0
        ),
        name="embed",
    )(place, source, got, *pieces, gain)


def gain_of(rows):
    wide = rows.astype(F32)
    return wide[0:1] + wide[1:2] + wide[2:3]


def head_norm(values):
    center = jnp.mean(values, axis=1, keepdims=True)
    spread = jnp.mean(values * values, axis=1, keepdims=True) - center * center
    inv = lax.rsqrt(spread + EPS)
    return (values - center) * inv, inv


def head_back(grad_hat, unit, inv, gain):
    t = grad_hat * gain
    mean_t = jnp.mean(t, axis=1, keepdims=True)
    second = jnp.mean(t * unit, axis=1, keepdims=True)
    return inv * (t - mean_t - unit * second)


def lanes_sum(v):
    total = v[:, :128]
    for k in range(1, v.shape[1] // 128):
        total = total + v[:, k * 128 : (k + 1) * 128]
    return total


def norm_kernel(place, e, pick, normed, values, ms_out, acc1, acc2):
    x = place[0]
    acc1[...] = jnp.zeros_like(acc1)
    acc2[...] = jnp.zeros_like(acc2)

    def sums(b, carry):
        wide = e[b, :ROWS, :].astype(F32)
        acc1[...] += lanes_sum(wide)
        acc2[...] += lanes_sum(wide * wide)
        return carry

    lax.fori_loop(0, 8, sums, 0)
    mean = jnp.sum(acc1[...], axis=1, keepdims=True) * (1.0 / D)
    square = jnp.sum(acc2[...], axis=1, keepdims=True) * (1.0 / D)
    scale = lax.rsqrt(square - mean * mean + EPS)
    lane = lax.broadcasted_iota(jnp.int32, (ROWS, 128), 1)
    ms_out[...] = jnp.where(lane == 0, mean, scale)

    def norm(b, carry):
        wide = e[b, :ROWS, :].astype(F32)
        gain = gain_of(e[b, ROWS:, :])
        normed[b] = ((wide - mean) * scale * gain).astype(BF16)
        return carry

    lax.fori_loop(0, 8, norm, 0)
    picked = dot(normed[2 * x], pick[0]) + dot(normed[2 * x + 1], pick[1])
    values[...] = picked.astype(BF16)


def norm_rows(place, blocks, pick):
    return pl.pallas_call(
        norm_kernel,
        out_shape=(
            jax.ShapeDtypeStruct((8, ROWS, FB), BF16),
            jax.ShapeDtypeStruct((ROWS, HW), BF16),
            jax.ShapeDtypeStruct((ROWS, 128), F32),
        ),
        in_specs=[pl.BlockSpec(memory_space=pltpu.SMEM)] + vmem(2),
        out_specs=tuple(vmem(3)),
        scratch_shapes=[pltpu.VMEM((ROWS, 128), F32), pltpu.VMEM((ROWS, 128), F32)],
        compiler_params=pltpu.CompilerParams(vmem_limit_bytes=24 * 2**20),
        cost_estimate=pl.CostEstimate(
            flops=4 * ROWS * FB * HW, bytes_accessed=12000000, transcendentals=0
        ),
        name="norm",
    )(place, blocks, pick)


def layer_kernel(*refs):
    place, facts, e_in, normed, values, ms = refs[:6]
    a_refs, b_refs = refs[6:11], refs[11:20]
    pick, packs, near, far, q_gain, k_gain = refs[20:26]
    att_here, att_near, att_far, own_out, other_out = refs[26:31]
    w, acc, grad, grad_v, acc1, acc2, cot, att, e, sems = refs[31:]
    x, y, z, c = place[0], place[1], place[2], place[3]
    first = pl.ds(0, HW)
    second = pl.ds(HW, HW)
    copies = []

    def go(src, dst):
        copies.append(pltpu.make_async_copy(src, dst, sems.at[len(copies)]))
        copies[-1].start()

    for core in range(NC):
        for k in range(3):
            yk = lax.rem(y + (0, NY - 1, 1)[k], NY)
            go(a_refs[k].at[:, core], w.at[2 * yk + core, :, :, first])
        for k in range(2):
            yk = lax.rem(y + 2, NY)
            go(a_refs[3 + k].at[:, core], w.at[2 * yk + core, pl.ds(4 * k, 4), :, first])
    for k in range(9):
        zk = lax.rem(z + (0, NZ - 1, 1, NZ - 2, 2, NZ - 3, 3, 4, 4)[k], NZ)
        rows = pl.ds(0, 8) if k < 7 else pl.ds(4 * (k - 7), 4)
        go(b_refs[k], w.at[rows, zk, :, second])
    go(e_in, e)
    acc[...] = jnp.zeros_like(acc)
    n_at = PATCH % 128
    counts = [facts[i, n_at] for i in range(NC * IMG_LOAD)]
    slots = [facts[i, n_at + 1] for i in range(NC * IMG_LOAD)]
    by_slot = (
        (packs[0, 0], packs[1, 1], near[1], near[3]),
        (packs[1, 0], near[0], near[2], far[...]),
    )
    for i, slot in enumerate(slots):
        rows = jnp.zeros((MOST, HW), F32)
        for k in range(REACH):
            piece = by_slot[i // IMG_LOAD][k].astype(F32)
            rows = jnp.where(slot == k, piece, rows)
        cot[i * MOST : (i + 1) * MOST, :] = rows.astype(BF16)
    for copy in copies[:-1]:
        copy.wait()

    def block(b):
        return w[b].reshape(FB, 2 * HW)

    def project(b, carry):
        acc[...] += dot(normed[b], block(b))
        return carry

    lax.fori_loop(0, 8, project, 0)

    inv_root = HD ** (-0.5)
    span = 2 * MOST
    row = lax.broadcasted_iota(jnp.int32, (span, span), 0)
    col = lax.broadcasted_iota(jnp.int32, (span, span), 1)
    qg, kg = q_gain[...], k_gain[...]
    masks = []
    for g in range(ROWS // span):
        n0, n1 = counts[2 * g], counts[2 * g + 1]
        top_r = jnp.where(row < MOST, n0, n1 + MOST)
        top_c = jnp.where(col < MOST, n0, n1 + MOST)
        same = jnp.where(row < MOST, 0, 1) == jnp.where(col < MOST, 0, 1)
        masks.append(((row < top_r) & (col < top_c) & same, row[:, :1] < top_r[:, :1]))
    for h in range(HC):
        cols = slice(h * HD, (h + 1) * HD)
        kcols = slice(HW + h * HD, HW + (h + 1) * HD)
        q_unit, q_inv = head_norm(acc[:, cols])
        k_unit, k_inv = head_norm(acc[:, kcols])
        q_hat = (q_unit * qg).astype(BF16)
        k_hat = (k_unit * kg).astype(BF16)
        gq, gk = [], []
        for g in range(ROWS // span):
            rows = slice(g * span, (g + 1) * span)
            allowed, live = masks[g]
            q, k, v, go = q_hat[rows], k_hat[rows], values[rows, cols], cot[rows, cols]
            scores = dot(q, k, NT) * inv_root
            raised = jnp.where(allowed, jnp.exp(scores), 0.0)
            totals = jnp.sum(raised, axis=1, keepdims=True)
            totals = jnp.where(live, totals, 1.0)
            probs = raised / totals
            low = probs.astype(BF16)
            att[rows, cols] = dot(low, v).astype(BF16)
            g_probs = dot(go, v, NT)
            grad_v[rows, cols] = dot(low, go, TN).astype(BF16)
            g_scores = probs * (g_probs - jnp.sum(probs * g_probs, axis=1, keepdims=True))
            g_low = (g_scores * inv_root).astype(BF16)
            gq.append(dot(g_low, k))
            gk.append(dot(g_low, q, TN))
        grad[:, cols] = head_back(jnp.concatenate(gq, axis=0), q_unit, q_inv, qg).astype(BF16)
        grad[:, kcols] = head_back(jnp.concatenate(gk, axis=0), k_unit, k_inv, kg).astype(BF16)

    goes = (
        ((att_here, 0), (att_here, 1), (att_near, 0), (att_near, 1)),
        ((att_here, 2), (att_near, 2), (att_near, 3), (att_far, 0)),
    )
    for core in range(NC):
        for k, (out, at) in enumerate(goes[core]):
            rows = jnp.zeros((MOST, HW), F32)
            for i in range(core * IMG_LOAD, (core + 1) * IMG_LOAD):
                piece = att[i * MOST : (i + 1) * MOST, :].astype(F32)
                rows = jnp.where(slots[i] == k, piece, rows)
            out[at] = rows.astype(BF16)

    acc1[...] = jnp.zeros_like(acc1)
    acc2[...] = jnp.zeros_like(acc2)
    mean, scale = ms[:, 0:1], ms[:, 1:2]

    def back(k, core, out, with_values):
        b = 2 * lax.rem(x + k, NX) + core
        part = dot(grad[...], block(b), NT)
        if with_values:
            part = part + dot(grad_v[...], pick[core], NT)
        out[k, :ROWS, :] = part.astype(BF16)
        t = part * gain_of(e[b, ROWS:, :])
        unit = (e[b, :ROWS, :].astype(F32) - mean) * scale
        acc1[...] += lanes_sum(t)
        acc2[...] += lanes_sum(t * unit)

    copies[-1].wait()
    for out, core in ((other_out, 1 - c), (own_out, c)):
        back(0, core, out, True)

        def step(k, carry, core=core, out=out):
            back(k, core, out, False)
            return carry

        lax.fori_loop(1, NX, step, 0)
    ones = jnp.ones((8, 128), F32)
    stats = []
    for part in (acc1, acc2):
        total = lax.dot_general(ones, part[...], NT, preferred_element_type=F32, precision=HIGH)
        stats.append(jnp.concatenate([total, jnp.zeros((8, FB - ROWS), F32)], axis=1))
    rows = stat_rows(stats[0][:1], stats[1][:1])
    for out in (own_out, other_out):
        for k in range(NX):
            out[k, ROWS:, :] = rows


def stat_rows(first, second):
    row = lax.broadcasted_iota(jnp.int32, (16, FB), 0)
    parts = []
    for v in (first, second):
        high = v.astype(BF16).astype(F32)
        parts += [high, v - high]
    out = jnp.zeros((16, FB), F32)
    for k in range(4):
        out = jnp.where(row == k, parts[k], out)
    return out.astype(BF16)


def stats_of(rows):
    wide = rows.astype(F32)
    return wide[0:1] + wide[1:2], wide[2:3] + wide[3:4]


def layer(place, facts, rows, a_pieces, b_pieces, pick, cot_pieces, q_gain, k_gain):
    hbm = [pl.BlockSpec(memory_space=pltpu.HBM)]
    smem = [pl.BlockSpec(memory_space=pltpu.SMEM)]
    flops = 4 * ROWS * D * 2 * HW
    return pl.pallas_call(
        layer_kernel,
        out_shape=(
            jax.ShapeDtypeStruct((3, MOST, HW), BF16),
            jax.ShapeDtypeStruct((4, MOST, HW), BF16),
            jax.ShapeDtypeStruct((1, MOST, HW), BF16),
            jax.ShapeDtypeStruct((NX, EROWS, FB), BF16),
            jax.ShapeDtypeStruct((NX, EROWS, FB), BF16),
        ),
        in_specs=smem * 2 + hbm + vmem(3) + hbm * 14 + vmem(6),
        out_specs=tuple(vmem(5)),
        scratch_shapes=[
            pltpu.VMEM((8, NZ, STRIP, 2 * HW), BF16),
            pltpu.VMEM((ROWS, 2 * HW), F32),
            pltpu.VMEM((ROWS, 2 * HW), BF16),
            pltpu.VMEM((ROWS, HW), BF16),
            pltpu.VMEM((ROWS, 128), F32),
            pltpu.VMEM((ROWS, 128), F32),
            pltpu.VMEM((ROWS, HW), BF16),
            pltpu.VMEM((ROWS, HW), BF16),
            pltpu.VMEM((8, EROWS, FB), BF16),
            pltpu.SemaphoreType.DMA((20,)),
        ],
        compiler_params=pltpu.CompilerParams(vmem_limit_bytes=40 * 2**20),
        cost_estimate=pl.CostEstimate(flops=flops, bytes_accessed=20000000, transcendentals=100000),
        name="layer",
    )(place, facts, *rows, *a_pieces, *b_pieces, pick, *cot_pieces, q_gain, k_gain)


def pair_kernel(own, got, *outs):
    for k, out in enumerate(outs):
        out[:ROWS, :] = (own[k, :ROWS, :].astype(F32) + got[k, :ROWS, :].astype(F32)).astype(BF16)
        a, b = stats_of(own[k, ROWS:, :]), stats_of(got[k, ROWS:, :])
        out[ROWS:, :] = stat_rows(a[0] + b[0], a[1] + b[1])


def pair_sum(own, got):
    return pl.pallas_call(
        pair_kernel,
        out_shape=(jax.ShapeDtypeStruct((EROWS, FB), BF16),) * NX,
        in_specs=vmem(2),
        out_specs=tuple(vmem(NX)),
        compiler_params=pltpu.CompilerParams(vmem_limit_bytes=16 * 2**20),
        cost_estimate=pl.CostEstimate(flops=1000000, bytes_accessed=6000000, transcendentals=0),
        name="pair_sum",
    )(own, got)


def embed_back_kernel(
    place, own, r1, r2, r3, e_own, ms, pix, own_out, send_out, full
):
    y = place[1]
    part = own[:ROWS, :].astype(F32)
    sums = stats_of(own[ROWS:, :])
    for ref in (r1, r2, r3):
        part = part + ref[:ROWS, :].astype(F32)
        more = stats_of(ref[ROWS:, :])
        sums = (sums[0] + more[0], sums[1] + more[1])
    mean, scale = ms[:, 0:1], ms[:, 1:2]
    gain = gain_of(e_own[ROWS:, :])
    chooser = jnp.where(lax.broadcasted_iota(jnp.int32, (8, 128), 0) == 0, 1.0 / D, 0.0)
    columns = []
    for v in sums:
        tall = jnp.broadcast_to(v[:, :ROWS], (8, ROWS))
        columns.append(
            lax.dot_general(tall, chooser, TN, preferred_element_type=F32, precision=HIGH)[:, :1]
        )
    t = part * gain
    unit = (e_own[:ROWS, :].astype(F32) - mean) * scale
    grad = (scale * (t - columns[0] - unit * columns[1])).astype(BF16)
    full[...] = dot(grad, pix[...], TN)
    for k in range(NY):
        at = pl.multiple_of(lax.rem(y + k, NY) * YROWS, YROWS)
        piece = full[pl.ds(at, YROWS), :]
        if k == 0:
            own_out[...] = piece
        else:
            send_out[k - 1] = piece.astype(BF16)


def embed_back(place, *args):
    return pl.pallas_call(
        embed_back_kernel,
        out_shape=(
            jax.ShapeDtypeStruct((YROWS, PATCH), F32),
            jax.ShapeDtypeStruct((NY - 1, YROWS, PATCH), BF16),
        ),
        in_specs=[pl.BlockSpec(memory_space=pltpu.SMEM)] + vmem(7),
        out_specs=tuple(vmem(2)),
        scratch_shapes=[pltpu.VMEM((FB, PATCH), F32)],
        compiler_params=pltpu.CompilerParams(vmem_limit_bytes=32 * 2**20),
        cost_estimate=pl.CostEstimate(
            flops=2 * ROWS * FB * PATCH, bytes_accessed=5000000, transcendentals=0
        ),
        name="embed_back",
    )(place, *args)


def per_device(
    pixels,
    patch_counts,
    pack_index,
    embed_weight,
    norm_gain,
    query_weight,
    key_weight,
    query_gain,
    key_gain,
    cotangent,
):
    x, y, z, c = [lax.axis_index(name) for name in ("x", "y", "z", "core")]
    d = (y * NZ + z) * NC + c
    place = jnp.stack([x, y, z, c]).astype(jnp.int32)

    strip = jnp.swapaxes(embed_weight.reshape(PATCH, PIECE), 0, 1)
    strip = by_core(z % 2, strip, z_swap(strip, 1), 0)
    sent, kept, source = prep(
        place, patch_counts, pack_index, query_weight, key_weight, cotangent, pixels
    )
    got = core_swap(sent)
    n_w = 2 * NC * PIECE
    shards = []
    for k in range(2):
        rows = slice(k * n_w, (k + 1) * n_w)
        mine = kept[rows].reshape(NC, 2 * PIECE, HW)
        shards.append(by_core(c, mine, got[rows].reshape(NC, 2 * PIECE, HW), 1))
    a0, b0 = shards

    after = lax.optimization_barrier
    a_own = lax.all_gather(a0, "z", axis=0, tiled=False)
    b_near = [y_shift(b0, -k) for k in range(1, NY)]
    for step in (2, 4):
        strip = by_core(z // step % 2, strip, z_swap(strip, step), 0)
    strip, b_near = after((strip, b_near))
    b_own = in_order(place, [b0] + b_near)
    embed_pieces = [strip] + [y_shift(strip, -k) for k in range(1, NY)]
    bl1, br1 = z_shift(b_own, 1), z_shift(b_own, -1)
    bl2, br2 = z_shift(bl1, 1), z_shift(br1, -1)
    bl3, br3 = z_shift(bl2, 1), z_shift(br2, -1)
    bl4, br4 = z_shift(bl3[:4], 1), z_shift(br3[4:], -1)
    a_low, a_high = y_shift(a_own, 1), y_shift(a_own, -1)
    a_pieces = [a_own, a_low, a_high, y_shift(a_low[:4], 1), y_shift(a_high[4:], -1)]
    b_pieces = [b_own, bl1, br1, bl2, br2, bl3, br3, bl4, br4]

    gain_here = jnp.where(
        c == 0, norm_gain.reshape(-1, NC, PIECE)[:, 0], norm_gain.reshape(-1, NC, PIECE)[:, 1]
    ).reshape(1, FB)
    e_own, pix, facts = embed(place, source, got, embed_pieces, gain_here)
    blocks = lax.all_gather(e_own, ("x", "core"), axis=0, tiled=False)

    kept_cot, got_cot, bl2 = after((kept[2 * n_w :], got[2 * n_w : 2 * n_w + PACK], bl2))
    packs = by_core(c, kept_cot[None], got_cot[None], 0)
    packs = packs.reshape(NC, REACH, MOST, HW)
    near = chip_shift(jnp.stack([packs[0, 1], packs[0, 2], packs[1, 2], packs[1, 3]]), -1)
    far = chip_shift(packs[0, 3], -2)

    column = jnp.arange(HW, dtype=jnp.int32)[None, None, :]
    feature = (c * HC + column // HD) * (D // HEADS) + column % HD
    at = (feature // (NC * PIECE)) * PIECE + feature % PIECE
    part = (feature // PIECE) % NC
    pick = (
        (jnp.arange(FB, dtype=jnp.int32)[None, :, None] == at)
        & (jnp.arange(NC, dtype=jnp.int32)[:, None, None] == part)
    ).astype(BF16)

    normed, values, ms = norm_rows(place, blocks, pick)
    att_here, att_near, att_far, own_grad, other_grad = layer(
        place,
        facts,
        (blocks, normed, values, ms),
        a_pieces,
        b_pieces,
        pick,
        (packs, near, far),
        query_gain.reshape(1, HD),
        key_gain.reshape(1, HD),
    )

    pair = pair_sum(own_grad, core_swap(other_grad))
    arrived = [x_shift(pair[k], k) for k in range(1, NX)]
    grad_own, grad_send = embed_back(place, pair[0], *arrived, e_own, ms, pix)
    total = grad_own
    for k in range(1, NY):
        total = total + y_shift(grad_send[k - 1], k).astype(F32)
    total = total.reshape(NZ, PIECE, PATCH)
    sent = total.astype(BF16)
    arrived = lax.all_to_all(sent, "z", 0, 0)
    embed_grad = jnp.sum(arrived.astype(F32), axis=0)
    embed_grad = jnp.swapaxes(embed_grad, 0, 1).reshape(PATCH, 1, PIECE)

    near = chip_shift(att_near, 1)
    far = chip_shift(att_far, 2)
    packs = jnp.concatenate(
        [att_here[0], near[2], near[0], far[0], att_here[2], att_here[1], near[3], near[1]], axis=0
    ).reshape(NC, PACK, HW)
    keep = jnp.where(c == 0, packs[0], packs[1])
    give = jnp.where(c == 0, packs[1], packs[0])
    attended = by_core(c, keep, core_swap(give), 1)
    return attended, embed_grad


def solution(mesh):
    chips = Mesh(mesh.devices.reshape(NY, NZ, NC, NX), ("y", "z", "core", "x"))
    dp = ("y", "z", "core")
    placed = (
        P(dp, None),
        P(dp),
        P(dp),
        P(None, "x", dp),
        P("x"),
        P(dp, "x"),
        P(dp, "x"),
        P(),
        P(),
        P(dp, "x"),
    )
    return jax.shard_map(
        per_device,
        mesh=chips,
        in_specs=placed,
        out_specs=(P(dp, "x"), P(None, "x", dp)),
        check_vma=False,
    )
```

```python
import functools

import jax
import jax.numpy as jnp
from jax import lax
from jax.experimental import pallas as pl
from jax.experimental.pallas import tpu as pltpu
from jax.sharding import Mesh
from jax.sharding import PartitionSpec as P

D = 6144
HEADS = 24
HD = 128
PATCH = 588
MOST = 48
IMG_LOAD = 3
REACH = 4
EPS = 1e-06

NY, NZ, NC, NX = 4, 8, 2, 4
NDP = NY * NZ * NC
FX = D // NX
FB = FX // NC
HC = HEADS // NX // NC
HW = HC * HD
ROWS = NC * IMG_LOAD * MOST
EROWS = ROWS + 16
STRIP = FB // NZ
PACK = REACH * MOST
PIECE = FX // NDP
YROWS = NZ * PIECE
NT = (((1,), (1,)), ((), ()))
TN = (((0,), (0,)), ((), ()))
F32 = jnp.float32
BF16 = jnp.bfloat16
HIGH = lax.Precision.HIGHEST


def dot(a, b, dims=(((1,), (0,)), ((), ()))):
    return lax.dot_general(a, b, dims, preferred_element_type=F32)


def ring(v, axis, n, k):
    return lax.ppermute(v, axis, [(i, (i + k) % n) for i in range(n)])


def core_swap(v):
    return ring(v, "core", NC, 1)


def z_shift(v, k):
    return ring(v, "z", NZ, k)


def z_swap(v, step):
    return lax.ppermute(v, "z", [(i, i ^ step) for i in range(NZ)])


def y_shift(v, k):
    return ring(v, "y", NY, k)


def x_shift(v, k):
    return ring(v, "x", NX, k)


def chip_shift(v, k):
    return ring(v, ("y", "z"), NY * NZ, k)


def by_core(core, mine, other, axis):
    return jnp.where(
        core == 0,
        jnp.concatenate([mine, other], axis=axis),
        jnp.concatenate([other, mine], axis=axis),
    )


def turn(pieces, start, axis):
    n = len(pieces)
    double = jnp.concatenate(list(pieces) + list(pieces), axis=axis)
    size = pieces[0].shape[axis]
    return lax.dynamic_slice_in_dim(double, start * size, n * size, axis=axis)


def vmem(n):
    return [pl.BlockSpec(memory_space=pltpu.VMEM)] * n


def regroup(rows):
    wide = rows.astype(F32)
    order = [wide[(2 * q + k) * PIECE : (2 * q + k + 1) * PIECE] for k in range(2) for q in range(2)]
    return jnp.concatenate(order, axis=0).astype(BF16)


def prep_kernel(
    place, counts, packs, wq_in, wk_in, cot_in, pix_in, send, kept, source, wq, wk, cot, pix, sems
):
    y, z, c = place[1], place[2], place[3]
    pairs = ((pix_in, pix), (wq_in, wq), (wk_in, wk), (cot_in, cot))
    copies = [pltpu.make_async_copy(a, b, sems.at[k]) for k, (a, b) in enumerate(pairs)]
    for copy in copies:
        copy.start()
    for copy in copies:
        copy.wait()
    d = (y * NZ + z) * NC + c
    lane = lax.broadcasted_iota(jnp.int32, (MOST, 2 * HW), 1)
    row = lax.broadcasted_iota(jnp.int32, (MOST, 2 * HW), 0)
    source[...] = jnp.zeros_like(source)
    source[:, :PATCH] = pix[...]
    for i in range(IMG_LOAD):
        rows = pl.ds(i * MOST, MOST)
        n = counts[i]
        slot = lax.rem(packs[i] - d + NDP, NDP)
        values = jnp.where(row < n, source[rows, :].astype(F32), 0.0)
        values = jnp.where(lane == PATCH, n.astype(F32), values)
        values = jnp.where(lane == PATCH + 1, slot.astype(F32), values)
        source[rows, :] = values.astype(BF16)

    n_w = 2 * NC * PIECE
    halves = (slice(0, HW), slice(HW, 2 * HW))
    for core in range(NC):

        @pl.when(c == core)
        def _(core=core):
            for k, w in enumerate((wq, wk)):
                kept[k * n_w : (k + 1) * n_w, :] = regroup(w[:, halves[core]])
                send[k * n_w : (k + 1) * n_w, :] = regroup(w[:, halves[1 - core]])
            kept[2 * n_w :, :] = cot[:, halves[core]]
            send[2 * n_w : 2 * n_w + PACK, :] = cot[:, halves[1 - core]]

    at = 2 * n_w + PACK
    for k in range(2):
        send[at + k * IMG_LOAD * MOST : at + (k + 1) * IMG_LOAD * MOST, :] = source[:, halves[k]]


def prep(place, counts, packs, wq, wk, cot, pix):
    n_w = 2 * NC * PIECE
    return pl.pallas_call(
        prep_kernel,
        out_shape=(
            jax.ShapeDtypeStruct((2 * n_w + PACK + 2 * IMG_LOAD * MOST, HW), BF16),
            jax.ShapeDtypeStruct((2 * n_w + PACK, HW), BF16),
            jax.ShapeDtypeStruct((IMG_LOAD * MOST, 2 * HW), BF16),
        ),
        in_specs=[pl.BlockSpec(memory_space=pltpu.SMEM)] * 3
        + [pl.BlockSpec(memory_space=pltpu.HBM)] * 4,
        out_specs=tuple(vmem(3)),
        scratch_shapes=[
            pltpu.VMEM(wq.shape, BF16),
            pltpu.VMEM(wk.shape, BF16),
            pltpu.VMEM(cot.shape, BF16),
            pltpu.VMEM(pix.shape, BF16),
            pltpu.SemaphoreType.DMA((4,)),
        ],
        compiler_params=pltpu.CompilerParams(vmem_limit_bytes=60 * 2**20),
        cost_estimate=pl.CostEstimate(flops=1000000, bytes_accessed=2000000, transcendentals=0),
        name="prep",
    )(place, counts, packs, wq, wk, cot, pix)


def order_kernel(place, *refs):
    pieces, out = refs[:-1], refs[-1]
    for k, piece in enumerate(pieces):
        out[pl.ds(2 * lax.rem(place[1] + k, NY), 2)] = piece[...]


def in_order(place, pieces):
    return pl.pallas_call(
        order_kernel,
        out_shape=jax.ShapeDtypeStruct((NY * NC, STRIP, HW), BF16),
        in_specs=[pl.BlockSpec(memory_space=pltpu.SMEM)] + vmem(len(pieces)),
        out_specs=pl.BlockSpec(memory_space=pltpu.VMEM),
        cost_estimate=pl.CostEstimate(flops=0, bytes_accessed=2000000, transcendentals=0),
        name="order",
    )(place, *pieces)


def embed_kernel(place, source, got, w0, w1, w2, w3, gain, out, pix, facts, weights):
    y, c = place[1], place[3]
    for k, piece in enumerate((w0, w1, w2, w3)):
        at = pl.multiple_of(lax.rem(y + k, NY) * YROWS, YROWS)
        weights[pl.ds(at, YROWS), :] = piece[...]
    half = IMG_LOAD * MOST
    at = 4 * NC * PIECE + PACK
    mine = source[...]
    other = jnp.concatenate([got[at : at + half, :], got[at + half : at + 2 * half, :]], axis=1)
    low = jnp.where(c == 0, mine, other)
    high = jnp.where(c == 0, other, mine)
    pix[:half, :] = low[:, :PATCH]
    pix[half:, :] = high[:, :PATCH]
    first = PATCH // 128 * 128
    for core, part in enumerate((low, high)):
        wide = part[:, first : first + 128].astype(F32)
        for i in range(IMG_LOAD):
            k = core * IMG_LOAD + i
            facts[k : k + 1, :] = wide[i * MOST : i * MOST + 1, :].astype(jnp.int32)
    facts[NC * IMG_LOAD :, :] = jnp.zeros((8 - NC * IMG_LOAD, 128), jnp.int32)
    out[:ROWS, :] = dot(pix[...], weights[...], NT).astype(BF16)
    full = gain[...]
    high = full.astype(BF16)
    rest = full - high.astype(F32)
    mid = rest.astype(BF16)
    low = (rest - mid.astype(F32)).astype(BF16)
    row = lax.broadcasted_iota(jnp.int32, (16, FB), 0)
    out[ROWS:, :] = jnp.where(
        row == 0,
        high.astype(F32),
        jnp.where(row == 1, mid.astype(F32), jnp.where(row == 2, low.astype(F32), 0.0)),
    ).astype(BF16)


def embed(place, source, got, pieces, gain):
    return pl.pallas_call(
        embed_kernel,
        out_shape=(
            jax.ShapeDtypeStruct((EROWS, FB), BF16),
            jax.ShapeDtypeStruct((ROWS, PATCH), BF16),
            jax.ShapeDtypeStruct((8, 128), jnp.int32),
        ),
        in_specs=[pl.BlockSpec(memory_space=pltpu.SMEM)] + vmem(7),
        out_specs=tuple(vmem(3)),
        scratch_shapes=[pltpu.VMEM((FB, PATCH), BF16)],
        compiler_params=pltpu.CompilerParams(vmem_limit_bytes=24 * 2**20),
        cost_estimate=pl.CostEstimate(
            flops=2 * ROWS * FB * PATCH, bytes_accessed=2000000, transcendentals=0
        ),
        name="embed",
    )(place, source, got, *pieces, gain)


def gain_of(rows):
    wide = rows.astype(F32)
    return wide[0:1] + wide[1:2] + wide[2:3]


def head_norm(values):
    center = jnp.mean(values, axis=1, keepdims=True)
    spread = jnp.mean(values * values, axis=1, keepdims=True) - center * center
    inv = lax.rsqrt(spread + EPS)
    return (values - center) * inv, inv


def head_back(grad_hat, unit, inv, gain):
    t = grad_hat * gain
    mean_t = jnp.mean(t, axis=1, keepdims=True)
    second = jnp.mean(t * unit, axis=1, keepdims=True)
    return inv * (t - mean_t - unit * second)


def lanes_sum(v):
    total = v[:, :128]
    for k in range(1, v.shape[1] // 128):
        total = total + v[:, k * 128 : (k + 1) * 128]
    return total


def layer_kernel(*refs):
    place, facts, e_in = refs[:3]
    a_refs, b_refs = refs[3:8], refs[8:17]
    pick, packs, near, far, q_gain, k_gain = refs[17:23]
    att_here, att_near, att_far, own_out, other_out, ms = refs[23:29]
    w, acc, grad, grad_v, acc1, acc2, cot, att, e, normed, values, sems, e_sems = refs[29:]
    x, y, z, c = place[0], place[1], place[2], place[3]
    first = pl.ds(0, HW)
    second = pl.ds(HW, HW)
    copies = []

    def fetch(b):
        return pltpu.make_async_copy(e_in.at[b], e.at[b], e_sems.at[b])

    for b in range(8):
        fetch(b).start()

    def go(src, dst):
        copies.append(pltpu.make_async_copy(src, dst, sems.at[len(copies)]))
        copies[-1].start()

    for core in range(NC):
        for k in range(3):
            yk = lax.rem(y + (0, NY - 1, 1)[k], NY)
            go(a_refs[k].at[:, core], w.at[2 * yk + core, :, :, first])
        for k in range(2):
            yk = lax.rem(y + 2, NY)
            go(a_refs[3 + k].at[:, core], w.at[2 * yk + core, pl.ds(4 * k, 4), :, first])
    for k in range(9):
        zk = lax.rem(z + (0, NZ - 1, 1, NZ - 2, 2, NZ - 3, 3, 4, 4)[k], NZ)
        rows = pl.ds(0, 8) if k < 7 else pl.ds(4 * (k - 7), 4)
        go(b_refs[k], w.at[rows, zk, :, second])
    acc[...] = jnp.zeros_like(acc)
    acc1[...] = jnp.zeros_like(acc1)
    acc2[...] = jnp.zeros_like(acc2)

    def sums(b, carry):
        fetch(b).wait()
        wide = e[b, :ROWS, :].astype(F32)
        acc1[...] += lanes_sum(wide)
        acc2[...] += lanes_sum(wide * wide)
        return carry

    lax.fori_loop(0, 8, sums, 0)
    mean = jnp.sum(acc1[...], axis=1, keepdims=True) * (1.0 / D)
    square = jnp.sum(acc2[...], axis=1, keepdims=True) * (1.0 / D)
    scale = lax.rsqrt(square - mean * mean + EPS)
    lane = lax.broadcasted_iota(jnp.int32, (ROWS, 128), 1)
    ms[...] = jnp.where(lane == 0, mean, scale)

    def norm(b, carry):
        wide = e[b, :ROWS, :].astype(F32)
        gain = gain_of(e[b, ROWS:, :])
        normed[b] = ((wide - mean) * scale * gain).astype(BF16)
        return carry

    lax.fori_loop(0, 8, norm, 0)
    picked = dot(normed[2 * x], pick[0]) + dot(normed[2 * x + 1], pick[1])
    values[...] = picked.astype(BF16)
    n_at = PATCH % 128
    counts = [facts[i, n_at] for i in range(NC * IMG_LOAD)]
    slots = [facts[i, n_at + 1] for i in range(NC * IMG_LOAD)]
    by_slot = (
        (packs[0, 0], packs[1, 1], near[1], near[3]),
        (packs[1, 0], near[0], near[2], far[...]),
    )
    for i, slot in enumerate(slots):
        rows = jnp.zeros((MOST, HW), F32)
        for k in range(REACH):
            piece = by_slot[i // IMG_LOAD][k].astype(F32)
            rows = jnp.where(slot == k, piece, rows)
        cot[i * MOST : (i + 1) * MOST, :] = rows.astype(BF16)
    for copy in copies:
        copy.wait()

    def block(b):
        return w[b].reshape(FB, 2 * HW)

    def project(b, carry):
        acc[...] += dot(normed[b], block(b))
        return carry

    lax.fori_loop(0, 8, project, 0)

    inv_root = HD ** (-0.5)
    span = 2 * MOST
    row = lax.broadcasted_iota(jnp.int32, (span, span), 0)
    col = lax.broadcasted_iota(jnp.int32, (span, span), 1)
    qg, kg = q_gain[...], k_gain[...]
    masks = []
    for g in range(ROWS // span):
        n0, n1 = counts[2 * g], counts[2 * g + 1]
        top_r = jnp.where(row < MOST, n0, n1 + MOST)
        top_c = jnp.where(col < MOST, n0, n1 + MOST)
        same = jnp.where(row < MOST, 0, 1) == jnp.where(col < MOST, 0, 1)
        masks.append(((row < top_r) & (col < top_c) & same, row[:, :1] < top_r[:, :1]))
    for h in range(HC):
        cols = slice(h * HD, (h + 1) * HD)
        kcols = slice(HW + h * HD, HW + (h + 1) * HD)
        q_unit, q_inv = head_norm(acc[:, cols])
        k_unit, k_inv = head_norm(acc[:, kcols])
        q_hat = (q_unit * qg).astype(BF16)
        k_hat = (k_unit * kg).astype(BF16)
        gq, gk = [], []
        for g in range(ROWS // span):
            rows = slice(g * span, (g + 1) * span)
            allowed, live = masks[g]
            q, k, v, go = q_hat[rows], k_hat[rows], values[rows, cols], cot[rows, cols]
            scores = dot(q, k, NT) * inv_root
            raised = jnp.where(allowed, jnp.exp(scores), 0.0)
            totals = jnp.sum(raised, axis=1, keepdims=True)
            totals = jnp.where(live, totals, 1.0)
            probs = raised / totals
            low = probs.astype(BF16)
            att[rows, cols] = dot(low, v).astype(BF16)
            g_probs = dot(go, v, NT)
            grad_v[rows, cols] = dot(low, go, TN).astype(BF16)
            g_scores = probs * (g_probs - jnp.sum(probs * g_probs, axis=1, keepdims=True))
            g_low = (g_scores * inv_root).astype(BF16)
            gq.append(dot(g_low, k))
            gk.append(dot(g_low, q, TN))
        grad[:, cols] = head_back(jnp.concatenate(gq, axis=0), q_unit, q_inv, qg).astype(BF16)
        grad[:, kcols] = head_back(jnp.concatenate(gk, axis=0), k_unit, k_inv, kg).astype(BF16)

    goes = (
        ((att_here, 0), (att_here, 1), (att_near, 0), (att_near, 1)),
        ((att_here, 2), (att_near, 2), (att_near, 3), (att_far, 0)),
    )
    for core in range(NC):
        for k, (out, at) in enumerate(goes[core]):
            rows = jnp.zeros((MOST, HW), F32)
            for i in range(core * IMG_LOAD, (core + 1) * IMG_LOAD):
                piece = att[i * MOST : (i + 1) * MOST, :].astype(F32)
                rows = jnp.where(slots[i] == k, piece, rows)
            out[at] = rows.astype(BF16)

    acc1[...] = jnp.zeros_like(acc1)
    acc2[...] = jnp.zeros_like(acc2)
    mean, scale = ms[:, 0:1], ms[:, 1:2]

    def back(k, core, out, with_values):
        b = 2 * lax.rem(x + k, NX) + core
        part = dot(grad[...], block(b), NT)
        if with_values:
            part = part + dot(grad_v[...], pick[core], NT)
        out[k, :ROWS, :] = part.astype(BF16)
        t = part * gain_of(e[b, ROWS:, :])
        unit = (e[b, :ROWS, :].astype(F32) - mean) * scale
        acc1[...] += lanes_sum(t)
        acc2[...] += lanes_sum(t * unit)

    for out, core in ((other_out, 1 - c), (own_out, c)):
        back(0, core, out, True)

        def step(k, carry, core=core, out=out):
            back(k, core, out, False)
            return carry

        lax.fori_loop(1, NX, step, 0)
    ones = jnp.ones((8, 128), F32)
    stats = []
    for part in (acc1, acc2):
        total = lax.dot_general(ones, part[...], NT, preferred_element_type=F32, precision=HIGH)
        stats.append(jnp.concatenate([total, jnp.zeros((8, FB - ROWS), F32)], axis=1))
    rows = stat_rows(stats[0][:1], stats[1][:1])
    for out in (own_out, other_out):
        for k in range(NX):
            out[k, ROWS:, :] = rows


def stat_rows(first, second):
    row = lax.broadcasted_iota(jnp.int32, (16, FB), 0)
    parts = []
    for v in (first, second):
        high = v.astype(BF16).astype(F32)
        parts += [high, v - high]
    out = jnp.zeros((16, FB), F32)
    for k in range(4):
        out = jnp.where(row == k, parts[k], out)
    return out.astype(BF16)


def stats_of(rows):
    wide = rows.astype(F32)
    return wide[0:1] + wide[1:2], wide[2:3] + wide[3:4]


def layer(place, facts, blocks, a_pieces, b_pieces, pick, cot_pieces, q_gain, k_gain):
    hbm = [pl.BlockSpec(memory_space=pltpu.HBM)]
    smem = [pl.BlockSpec(memory_space=pltpu.SMEM)]
    flops = 4 * ROWS * D * 2 * HW
    return pl.pallas_call(
        layer_kernel,
        out_shape=(
            jax.ShapeDtypeStruct((3, MOST, HW), BF16),
            jax.ShapeDtypeStruct((4, MOST, HW), BF16),
            jax.ShapeDtypeStruct((1, MOST, HW), BF16),
            jax.ShapeDtypeStruct((NX, EROWS, FB), BF16),
            jax.ShapeDtypeStruct((NX, EROWS, FB), BF16),
            jax.ShapeDtypeStruct((ROWS, 128), F32),
        ),
        in_specs=smem * 2 + hbm * 15 + vmem(6),
        out_specs=tuple(vmem(6)),
        scratch_shapes=[
            pltpu.VMEM((8, NZ, STRIP, 2 * HW), BF16),
            pltpu.VMEM((ROWS, 2 * HW), F32),
            pltpu.VMEM((ROWS, 2 * HW), BF16),
            pltpu.VMEM((ROWS, HW), BF16),
            pltpu.VMEM((ROWS, 128), F32),
            pltpu.VMEM((ROWS, 128), F32),
            pltpu.VMEM((ROWS, HW), BF16),
            pltpu.VMEM((ROWS, HW), BF16),
            pltpu.VMEM((8, EROWS, FB), BF16),
            pltpu.VMEM((8, ROWS, FB), BF16),
            pltpu.VMEM((ROWS, HW), BF16),
            pltpu.SemaphoreType.DMA((19,)),
            pltpu.SemaphoreType.DMA((8,)),
        ],
        compiler_params=pltpu.CompilerParams(vmem_limit_bytes=60 * 2**20),
        cost_estimate=pl.CostEstimate(flops=flops, bytes_accessed=20000000, transcendentals=100000),
        name="layer",
    )(place, facts, blocks, *a_pieces, *b_pieces, pick, *cot_pieces, q_gain, k_gain)


def pair_kernel(own, got, *outs):
    for k, out in enumerate(outs):
        out[:ROWS, :] = (own[k, :ROWS, :].astype(F32) + got[k, :ROWS, :].astype(F32)).astype(BF16)
        a, b = stats_of(own[k, ROWS:, :]), stats_of(got[k, ROWS:, :])
        out[ROWS:, :] = stat_rows(a[0] + b[0], a[1] + b[1])


def pair_sum(own, got):
    return pl.pallas_call(
        pair_kernel,
        out_shape=(jax.ShapeDtypeStruct((EROWS, FB), BF16),) * NX,
        in_specs=vmem(2),
        out_specs=tuple(vmem(NX)),
        compiler_params=pltpu.CompilerParams(vmem_limit_bytes=16 * 2**20),
        cost_estimate=pl.CostEstimate(flops=1000000, bytes_accessed=6000000, transcendentals=0),
        name="pair_sum",
    )(own, got)


def embed_back_kernel(
    place, own, r1, r2, r3, e_own, ms, pix, own_out, send_out, full
):
    y = place[1]
    part = own[:ROWS, :].astype(F32)
    sums = stats_of(own[ROWS:, :])
    for ref in (r1, r2, r3):
        part = part + ref[:ROWS, :].astype(F32)
        more = stats_of(ref[ROWS:, :])
        sums = (sums[0] + more[0], sums[1] + more[1])
    mean, scale = ms[:, 0:1], ms[:, 1:2]
    gain = gain_of(e_own[ROWS:, :])
    chooser = jnp.where(lax.broadcasted_iota(jnp.int32, (8, 128), 0) == 0, 1.0 / D, 0.0)
    columns = []
    for v in sums:
        tall = jnp.broadcast_to(v[:, :ROWS], (8, ROWS))
        columns.append(
            lax.dot_general(tall, chooser, TN, preferred_element_type=F32, precision=HIGH)[:, :1]
        )
    t = part * gain
    unit = (e_own[:ROWS, :].astype(F32) - mean) * scale
    grad = (scale * (t - columns[0] - unit * columns[1])).astype(BF16)
    full[...] = dot(grad, pix[...], TN)
    for k in range(NY):
        at = pl.multiple_of(lax.rem(y + k, NY) * YROWS, YROWS)
        piece = full[pl.ds(at, YROWS), :]
        if k == 0:
            own_out[...] = piece
        else:
            send_out[k - 1] = piece.astype(BF16)


def embed_back(place, *args):
    return pl.pallas_call(
        embed_back_kernel,
        out_shape=(
            jax.ShapeDtypeStruct((YROWS, PATCH), F32),
            jax.ShapeDtypeStruct((NY - 1, YROWS, PATCH), BF16),
        ),
        in_specs=[pl.BlockSpec(memory_space=pltpu.SMEM)] + vmem(7),
        out_specs=tuple(vmem(2)),
        scratch_shapes=[pltpu.VMEM((FB, PATCH), F32)],
        compiler_params=pltpu.CompilerParams(vmem_limit_bytes=32 * 2**20),
        cost_estimate=pl.CostEstimate(
            flops=2 * ROWS * FB * PATCH, bytes_accessed=5000000, transcendentals=0
        ),
        name="embed_back",
    )(place, *args)


def per_device(
    pixels,
    patch_counts,
    pack_index,
    embed_weight,
    norm_gain,
    query_weight,
    key_weight,
    query_gain,
    key_gain,
    cotangent,
):
    x, y, z, c = [lax.axis_index(name) for name in ("x", "y", "z", "core")]
    d = (y * NZ + z) * NC + c
    place = jnp.stack([x, y, z, c]).astype(jnp.int32)

    strip = jnp.swapaxes(embed_weight.reshape(PATCH, PIECE), 0, 1)
    strip = by_core(z % 2, strip, z_swap(strip, 1), 0)
    sent, kept, source = prep(
        place, patch_counts, pack_index, query_weight, key_weight, cotangent, pixels
    )
    got = core_swap(sent)
    n_w = 2 * NC * PIECE
    shards = []
    for k in range(2):
        rows = slice(k * n_w, (k + 1) * n_w)
        mine = kept[rows].reshape(NC, 2 * PIECE, HW)
        shards.append(by_core(c, mine, got[rows].reshape(NC, 2 * PIECE, HW), 1))
    a0, b0 = shards

    after = lax.optimization_barrier
    a_own = lax.all_gather(a0, "z", axis=0, tiled=False)
    b_near = [y_shift(b0, -k) for k in range(1, NY)]
    for step in (2, 4):
        strip = by_core(z // step % 2, strip, z_swap(strip, step), 0)
    strip, b_near = after((strip, b_near))
    b_own = in_order(place, [b0] + b_near)
    embed_pieces = [strip] + [y_shift(strip, -k) for k in range(1, NY)]
    bl1, br1 = z_shift(b_own, 1), z_shift(b_own, -1)
    bl2, br2 = z_shift(bl1, 1), z_shift(br1, -1)
    bl3, br3 = z_shift(bl2, 1), z_shift(br2, -1)
    bl4, br4 = z_shift(bl3[:4], 1), z_shift(br3[4:], -1)
    a_low, a_high = y_shift(a_own, 1), y_shift(a_own, -1)
    a_pieces = [a_own, a_low, a_high, y_shift(a_low[:4], 1), y_shift(a_high[4:], -1)]
    b_pieces = [b_own, bl1, br1, bl2, br2, bl3, br3, bl4, br4]

    gain_here = jnp.where(
        c == 0, norm_gain.reshape(-1, NC, PIECE)[:, 0], norm_gain.reshape(-1, NC, PIECE)[:, 1]
    ).reshape(1, FB)
    e_own, pix, facts = embed(place, source, got, embed_pieces, gain_here)
    blocks = lax.all_gather(e_own, ("x", "core"), axis=0, tiled=False)

    kept_cot, got_cot, bl2 = after((kept[2 * n_w :], got[2 * n_w : 2 * n_w + PACK], bl2))
    packs = by_core(c, kept_cot[None], got_cot[None], 0)
    packs = packs.reshape(NC, REACH, MOST, HW)
    near = chip_shift(jnp.stack([packs[0, 1], packs[0, 2], packs[1, 2], packs[1, 3]]), -1)
    far = chip_shift(packs[0, 3], -2)

    column = jnp.arange(HW, dtype=jnp.int32)[None, None, :]
    feature = (c * HC + column // HD) * (D // HEADS) + column % HD
    at = (feature // (NC * PIECE)) * PIECE + feature % PIECE
    part = (feature // PIECE) % NC
    pick = (
        (jnp.arange(FB, dtype=jnp.int32)[None, :, None] == at)
        & (jnp.arange(NC, dtype=jnp.int32)[:, None, None] == part)
    ).astype(BF16)

    att_here, att_near, att_far, own_grad, other_grad, ms = layer(
        place,
        facts,
        blocks,
        a_pieces,
        b_pieces,
        pick,
        (packs, near, far),
        query_gain.reshape(1, HD),
        key_gain.reshape(1, HD),
    )

    pair = pair_sum(own_grad, core_swap(other_grad))
    arrived = [x_shift(pair[k], k) for k in range(1, NX)]
    grad_own, grad_send = embed_back(place, pair[0], *arrived, e_own, ms, pix)
    total = grad_own
    for k in range(1, NY):
        total = total + y_shift(grad_send[k - 1], k).astype(F32)
    total = total.reshape(NZ, PIECE, PATCH)
    sent = total.astype(BF16)
    arrived = lax.all_to_all(sent, "z", 0, 0)
    embed_grad = jnp.sum(arrived.astype(F32), axis=0)
    embed_grad = jnp.swapaxes(embed_grad, 0, 1).reshape(PATCH, 1, PIECE)

    near = chip_shift(att_near, 1)
    far = chip_shift(att_far, 2)
    packs = jnp.concatenate(
        [att_here[0], near[2], near[0], far[0], att_here[2], att_here[1], near[3], near[1]], axis=0
    ).reshape(NC, PACK, HW)
    keep = jnp.where(c == 0, packs[0], packs[1])
    give = jnp.where(c == 0, packs[1], packs[0])
    attended = by_core(c, keep, core_swap(give), 1)
    return attended, embed_grad


def solution(mesh):
    chips = Mesh(mesh.devices.reshape(NY, NZ, NC, NX), ("y", "z", "core", "x"))
    dp = ("y", "z", "core")
    placed = (
        P(dp, None),
        P(dp),
        P(dp),
        P(None, "x", dp),
        P("x"),
        P(dp, "x"),
        P(dp, "x"),
        P(),
        P(),
        P(dp, "x"),
    )
    return jax.shard_map(
        per_device,
        mesh=chips,
        in_specs=placed,
        out_specs=(P(dp, "x"), P(None, "x", dp)),
        check_vma=False,
    )
```

```python
import functools

import jax
import jax.numpy as jnp
from jax import lax
from jax.experimental import pallas as pl
from jax.experimental.pallas import tpu as pltpu
from jax.sharding import Mesh
from jax.sharding import PartitionSpec as P

D = 6144
HEADS = 24
HD = 128
PATCH = 588
MOST = 48
IMG_LOAD = 3
REACH = 4
EPS = 1e-06

NY, NZ, NC, NX = 4, 8, 2, 4
NDP = NY * NZ * NC
FX = D // NX
FB = FX // NC
HC = HEADS // NX // NC
HW = HC * HD
ROWS = NC * IMG_LOAD * MOST
EROWS = ROWS + 16
STRIP = FB // NZ
PACK = REACH * MOST
PIECE = FX // NDP
YROWS = NZ * PIECE
NT = (((1,), (1,)), ((), ()))
TN = (((0,), (0,)), ((), ()))
F32 = jnp.float32
BF16 = jnp.bfloat16
HIGH = lax.Precision.HIGHEST


def dot(a, b, dims=(((1,), (0,)), ((), ()))):
    return lax.dot_general(a, b, dims, preferred_element_type=F32)


def ring(v, axis, n, k):
    return lax.ppermute(v, axis, [(i, (i + k) % n) for i in range(n)])


def core_swap(v):
    return ring(v, "core", NC, 1)


def z_shift(v, k):
    return ring(v, "z", NZ, k)


def z_swap(v, step):
    return lax.ppermute(v, "z", [(i, i ^ step) for i in range(NZ)])


def y_shift(v, k):
    return ring(v, "y", NY, k)


def x_shift(v, k):
    return ring(v, "x", NX, k)


def chip_shift(v, k):
    return ring(v, ("y", "z"), NY * NZ, k)


def by_core(core, mine, other, axis):
    return jnp.where(
        core == 0,
        jnp.concatenate([mine, other], axis=axis),
        jnp.concatenate([other, mine], axis=axis),
    )


def turn(pieces, start, axis):
    n = len(pieces)
    double = jnp.concatenate(list(pieces) + list(pieces), axis=axis)
    size = pieces[0].shape[axis]
    return lax.dynamic_slice_in_dim(double, start * size, n * size, axis=axis)


def vmem(n):
    return [pl.BlockSpec(memory_space=pltpu.VMEM)] * n


def regroup(rows):
    wide = rows.astype(F32)
    order = [wide[(2 * q + k) * PIECE : (2 * q + k + 1) * PIECE] for k in range(2) for q in range(2)]
    return jnp.concatenate(order, axis=0).astype(BF16)


def prep_kernel(
    place, counts, packs, wq_in, wk_in, cot_in, pix_in, send, kept, source, wq, wk, cot, pix, sems
):
    y, z, c = place[1], place[2], place[3]
    pairs = ((pix_in, pix), (wq_in, wq), (wk_in, wk), (cot_in, cot))
    copies = [pltpu.make_async_copy(a, b, sems.at[k]) for k, (a, b) in enumerate(pairs)]
    for copy in copies:
        copy.start()
    for copy in copies:
        copy.wait()
    d = (y * NZ + z) * NC + c
    lane = lax.broadcasted_iota(jnp.int32, (MOST, 2 * HW), 1)
    row = lax.broadcasted_iota(jnp.int32, (MOST, 2 * HW), 0)
    source[...] = jnp.zeros_like(source)
    source[:, :PATCH] = pix[...]
    for i in range(IMG_LOAD):
        rows = pl.ds(i * MOST, MOST)
        n = counts[i]
        slot = lax.rem(packs[i] - d + NDP, NDP)
        values = jnp.where(row < n, source[rows, :].astype(F32), 0.0)
        values = jnp.where(lane == PATCH, n.astype(F32), values)
        values = jnp.where(lane == PATCH + 1, slot.astype(F32), values)
        source[rows, :] = values.astype(BF16)

    n_w = 2 * NC * PIECE
    halves = (slice(0, HW), slice(HW, 2 * HW))
    for core in range(NC):

        @pl.when(c == core)
        def _(core=core):
            for k, w in enumerate((wq, wk)):
                kept[k * n_w : (k + 1) * n_w, :] = regroup(w[:, halves[core]])
                send[k * n_w : (k + 1) * n_w, :] = regroup(w[:, halves[1 - core]])
            kept[2 * n_w :, :] = cot[:, halves[core]]
            send[2 * n_w : 2 * n_w + PACK, :] = cot[:, halves[1 - core]]

    at = 2 * n_w + PACK
    for k in range(2):
        send[at + k * IMG_LOAD * MOST : at + (k + 1) * IMG_LOAD * MOST, :] = source[:, halves[k]]


def prep(place, counts, packs, wq, wk, cot, pix):
    n_w = 2 * NC * PIECE
    return pl.pallas_call(
        prep_kernel,
        out_shape=(
            jax.ShapeDtypeStruct((2 * n_w + PACK + 2 * IMG_LOAD * MOST, HW), BF16),
            jax.ShapeDtypeStruct((2 * n_w + PACK, HW), BF16),
            jax.ShapeDtypeStruct((IMG_LOAD * MOST, 2 * HW), BF16),
        ),
        in_specs=[pl.BlockSpec(memory_space=pltpu.SMEM)] * 3
        + [pl.BlockSpec(memory_space=pltpu.HBM)] * 4,
        out_specs=tuple(vmem(3)),
        scratch_shapes=[
            pltpu.VMEM(wq.shape, BF16),
            pltpu.VMEM(wk.shape, BF16),
            pltpu.VMEM(cot.shape, BF16),
            pltpu.VMEM(pix.shape, BF16),
            pltpu.SemaphoreType.DMA((4,)),
        ],
        compiler_params=pltpu.CompilerParams(vmem_limit_bytes=60 * 2**20),
        cost_estimate=pl.CostEstimate(flops=1000000, bytes_accessed=2000000, transcendentals=0),
        name="prep",
    )(place, counts, packs, wq, wk, cot, pix)


def order_kernel(place, *refs):
    pieces, out = refs[:-1], refs[-1]
    for k, piece in enumerate(pieces):
        out[pl.ds(2 * lax.rem(place[1] + k, NY), 2)] = piece[...]


def in_order(place, pieces):
    return pl.pallas_call(
        order_kernel,
        out_shape=jax.ShapeDtypeStruct((NY * NC, STRIP, HW), BF16),
        in_specs=[pl.BlockSpec(memory_space=pltpu.SMEM)] + vmem(len(pieces)),
        out_specs=pl.BlockSpec(memory_space=pltpu.VMEM),
        cost_estimate=pl.CostEstimate(flops=0, bytes_accessed=2000000, transcendentals=0),
        name="order",
    )(place, *pieces)


def embed_kernel(place, source, got, w0, w1, w2, w3, gain, out, pix, facts, weights):
    y, c = place[1], place[3]
    for k, piece in enumerate((w0, w1, w2, w3)):
        at = pl.multiple_of(lax.rem(y + k, NY) * YROWS, YROWS)
        weights[pl.ds(at, YROWS), :] = piece[...]
    half = IMG_LOAD * MOST
    at = 4 * NC * PIECE + PACK
    mine = source[...]
    other = jnp.concatenate([got[at : at + half, :], got[at + half : at + 2 * half, :]], axis=1)
    low = jnp.where(c == 0, mine, other)
    high = jnp.where(c == 0, other, mine)
    pix[:half, :] = low[:, :PATCH]
    pix[half:, :] = high[:, :PATCH]
    first = PATCH // 128 * 128
    for core, part in enumerate((low, high)):
        wide = part[:, first : first + 128].astype(F32)
        for i in range(IMG_LOAD):
            k = core * IMG_LOAD + i
            facts[k : k + 1, :] = wide[i * MOST : i * MOST + 1, :].astype(jnp.int32)
    facts[NC * IMG_LOAD :, :] = jnp.zeros((8 - NC * IMG_LOAD, 128), jnp.int32)
    out[:ROWS, :] = dot(pix[...], weights[...], NT).astype(BF16)
    full = gain[...]
    high = full.astype(BF16)
    rest = full - high.astype(F32)
    mid = rest.astype(BF16)
    low = (rest - mid.astype(F32)).astype(BF16)
    row = lax.broadcasted_iota(jnp.int32, (16, FB), 0)
    out[ROWS:, :] = jnp.where(
        row == 0,
        high.astype(F32),
        jnp.where(row == 1, mid.astype(F32), jnp.where(row == 2, low.astype(F32), 0.0)),
    ).astype(BF16)


def embed(place, source, got, pieces, gain):
    return pl.pallas_call(
        embed_kernel,
        out_shape=(
            jax.ShapeDtypeStruct((EROWS, FB), BF16),
            jax.ShapeDtypeStruct((ROWS, PATCH), BF16),
            jax.ShapeDtypeStruct((8, 128), jnp.int32),
        ),
        in_specs=[pl.BlockSpec(memory_space=pltpu.SMEM)] + vmem(7),
        out_specs=tuple(vmem(3)),
        scratch_shapes=[pltpu.VMEM((FB, PATCH), BF16)],
        compiler_params=pltpu.CompilerParams(vmem_limit_bytes=24 * 2**20),
        cost_estimate=pl.CostEstimate(
            flops=2 * ROWS * FB * PATCH, bytes_accessed=2000000, transcendentals=0
        ),
        name="embed",
    )(place, source, got, *pieces, gain)


def gain_of(rows):
    wide = rows.astype(F32)
    return wide[0:1] + wide[1:2] + wide[2:3]


def head_norm(values):
    center = jnp.mean(values, axis=1, keepdims=True)
    spread = jnp.mean(values * values, axis=1, keepdims=True) - center * center
    inv = lax.rsqrt(spread + EPS)
    return (values - center) * inv, inv


def head_back(grad_hat, unit, inv, gain):
    t = grad_hat * gain
    mean_t = jnp.mean(t, axis=1, keepdims=True)
    second = jnp.mean(t * unit, axis=1, keepdims=True)
    return inv * (t - mean_t - unit * second)


def lanes_sum(v):
    total = v[:, :128]
    for k in range(1, v.shape[1] // 128):
        total = total + v[:, k * 128 : (k + 1) * 128]
    return total


def layer_kernel(*refs):
    place, facts, e_in = refs[:3]
    a_refs, b_refs = refs[3:8], refs[8:17]
    pick, packs, near, far, q_gain, k_gain = refs[17:23]
    att_here, att_near, att_far, own_out, other_out, ms = refs[23:29]
    w, acc, grad, grad_v, acc1, acc2, cot, att, e, normed, values, sems, e_sems = refs[29:]
    x, y, z, c = place[0], place[1], place[2], place[3]
    first = pl.ds(0, HW)
    second = pl.ds(HW, HW)
    copies = []

    def fetch(b):
        return pltpu.make_async_copy(e_in.at[b], e.at[b], e_sems.at[b])

    for b in range(8):
        fetch(b).start()

    def go(src, dst):
        copies.append(pltpu.make_async_copy(src, dst, sems.at[len(copies)]))
        copies[-1].start()

    for core in range(NC):
        for k in range(3):
            yk = lax.rem(y + (0, NY - 1, 1)[k], NY)
            go(a_refs[k].at[:, core], w.at[2 * yk + core, :, :, first])
        for k in range(2):
            yk = lax.rem(y + 2, NY)
            go(a_refs[3 + k].at[:, core], w.at[2 * yk + core, pl.ds(4 * k, 4), :, first])
    for k in range(9):
        zk = lax.rem(z + (0, NZ - 1, 1, NZ - 2, 2, NZ - 3, 3, 4, 4)[k], NZ)
        rows = pl.ds(0, 8) if k < 7 else pl.ds(4 * (k - 7), 4)
        go(b_refs[k], w.at[rows, zk, :, second])
    acc[...] = jnp.zeros_like(acc)
    acc1[...] = jnp.zeros_like(acc1)
    acc2[...] = jnp.zeros_like(acc2)

    def sums(b, carry):
        fetch(b).wait()
        wide = e[b, :ROWS, :].astype(F32)
        acc1[...] += lanes_sum(wide)
        acc2[...] += lanes_sum(wide * wide)
        return carry

    lax.fori_loop(0, 8, sums, 0)
    mean = jnp.sum(acc1[...], axis=1, keepdims=True) * (1.0 / D)
    square = jnp.sum(acc2[...], axis=1, keepdims=True) * (1.0 / D)
    scale = lax.rsqrt(square - mean * mean + EPS)
    lane = lax.broadcasted_iota(jnp.int32, (ROWS, 128), 1)
    ms[...] = jnp.where(lane == 0, mean, scale)

    def norm(b, carry):
        wide = e[b, :ROWS, :].astype(F32)
        gain = gain_of(e[b, ROWS:, :])
        normed[b] = ((wide - mean) * scale * gain).astype(BF16)
        return carry

    lax.fori_loop(0, 8, norm, 0)
    picked = dot(normed[2 * x], pick[0]) + dot(normed[2 * x + 1], pick[1])
    values[...] = picked.astype(BF16)
    n_at = PATCH % 128
    counts = [facts[i, n_at] for i in range(NC * IMG_LOAD)]
    slots = [facts[i, n_at + 1] for i in range(NC * IMG_LOAD)]
    by_slot = (
        (packs[0, 0], packs[1, 1], near[1], near[3]),
        (packs[1, 0], near[0], near[2], far[...]),
    )
    for i, slot in enumerate(slots):
        rows = jnp.zeros((MOST, HW), F32)
        for k in range(REACH):
            piece = by_slot[i // IMG_LOAD][k].astype(F32)
            rows = jnp.where(slot == k, piece, rows)
        cot[i * MOST : (i + 1) * MOST, :] = rows.astype(BF16)
    for copy in copies:
        copy.wait()

    def block(b):
        return w[b].reshape(FB, 2 * HW)

    def project(b, carry):
        acc[...] += dot(normed[b], block(b))
        return carry

    lax.fori_loop(0, 8, project, 0)

    inv_root = HD ** (-0.5)
    span = 2 * MOST
    row = lax.broadcasted_iota(jnp.int32, (span, span), 0)
    col = lax.broadcasted_iota(jnp.int32, (span, span), 1)
    qg, kg = q_gain[...], k_gain[...]
    masks = []
    for g in range(ROWS // span):
        n0, n1 = counts[2 * g], counts[2 * g + 1]
        top_r = jnp.where(row < MOST, n0, n1 + MOST)
        top_c = jnp.where(col < MOST, n0, n1 + MOST)
        same = jnp.where(row < MOST, 0, 1) == jnp.where(col < MOST, 0, 1)
        masks.append(((row < top_r) & (col < top_c) & same, row[:, :1] < top_r[:, :1]))
    for h in range(HC):
        cols = slice(h * HD, (h + 1) * HD)
        kcols = slice(HW + h * HD, HW + (h + 1) * HD)
        q_unit, q_inv = head_norm(acc[:, cols])
        k_unit, k_inv = head_norm(acc[:, kcols])
        q_hat = (q_unit * qg).astype(BF16)
        k_hat = (k_unit * kg).astype(BF16)
        gq, gk = [], []
        for g in range(ROWS // span):
            rows = slice(g * span, (g + 1) * span)
            allowed, live = masks[g]
            q, k, v, go = q_hat[rows], k_hat[rows], values[rows, cols], cot[rows, cols]
            scores = dot(q, k, NT) * inv_root
            raised = jnp.where(allowed, jnp.exp(scores), 0.0)
            totals = jnp.sum(raised, axis=1, keepdims=True)
            totals = jnp.where(live, totals, 1.0)
            probs = raised / totals
            low = probs.astype(BF16)
            att[rows, cols] = dot(low, v).astype(BF16)
            g_probs = dot(go, v, NT)
            grad_v[rows, cols] = dot(low, go, TN).astype(BF16)
            g_scores = probs * (g_probs - jnp.sum(probs * g_probs, axis=1, keepdims=True))
            g_low = (g_scores * inv_root).astype(BF16)
            gq.append(dot(g_low, k))
            gk.append(dot(g_low, q, TN))
        grad[:, cols] = head_back(jnp.concatenate(gq, axis=0), q_unit, q_inv, qg).astype(BF16)
        grad[:, kcols] = head_back(jnp.concatenate(gk, axis=0), k_unit, k_inv, kg).astype(BF16)

    goes = (
        ((att_here, 0), (att_here, 1), (att_near, 0), (att_near, 1)),
        ((att_here, 2), (att_near, 2), (att_near, 3), (att_far, 0)),
    )
    for core in range(NC):
        for k, (out, at) in enumerate(goes[core]):
            rows = jnp.zeros((MOST, HW), F32)
            for i in range(core * IMG_LOAD, (core + 1) * IMG_LOAD):
                piece = att[i * MOST : (i + 1) * MOST, :].astype(F32)
                rows = jnp.where(slots[i] == k, piece, rows)
            out[at] = rows.astype(BF16)

    acc1[...] = jnp.zeros_like(acc1)
    acc2[...] = jnp.zeros_like(acc2)
    mean, scale = ms[:, 0:1], ms[:, 1:2]

    def back(k, core, out, with_values):
        b = 2 * lax.rem(x + k, NX) + core
        part = dot(grad[...], block(b), NT)
        if with_values:
            part = part + dot(grad_v[...], pick[core], NT)
        out[k, :ROWS, :] = part.astype(BF16)
        t = part * gain_of(e[b, ROWS:, :])
        unit = (e[b, :ROWS, :].astype(F32) - mean) * scale
        acc1[...] += lanes_sum(t)
        acc2[...] += lanes_sum(t * unit)

    for out, core in ((other_out, 1 - c), (own_out, c)):
        back(0, core, out, True)

        def step(k, carry, core=core, out=out):
            back(k, core, out, False)
            return carry

        lax.fori_loop(1, NX, step, 0)
    ones = jnp.ones((8, 128), F32)
    stats = []
    for part in (acc1, acc2):
        total = lax.dot_general(ones, part[...], NT, preferred_element_type=F32, precision=HIGH)
        stats.append(jnp.concatenate([total, jnp.zeros((8, FB - ROWS), F32)], axis=1))
    rows = stat_rows(stats[0][:1], stats[1][:1])
    for out in (own_out, other_out):
        for k in range(NX):
            out[k, ROWS:, :] = rows


def stat_rows(first, second):
    row = lax.broadcasted_iota(jnp.int32, (16, FB), 0)
    parts = []
    for v in (first, second):
        high = v.astype(BF16).astype(F32)
        parts += [high, v - high]
    out = jnp.zeros((16, FB), F32)
    for k in range(4):
        out = jnp.where(row == k, parts[k], out)
    return out.astype(BF16)


def stats_of(rows):
    wide = rows.astype(F32)
    return wide[0:1] + wide[1:2], wide[2:3] + wide[3:4]


def layer(place, facts, blocks, a_pieces, b_pieces, pick, cot_pieces, q_gain, k_gain):
    hbm = [pl.BlockSpec(memory_space=pltpu.HBM)]
    smem = [pl.BlockSpec(memory_space=pltpu.SMEM)]
    flops = 4 * ROWS * D * 2 * HW
    return pl.pallas_call(
        layer_kernel,
        out_shape=(
            jax.ShapeDtypeStruct((3, MOST, HW), BF16),
            jax.ShapeDtypeStruct((4, MOST, HW), BF16),
            jax.ShapeDtypeStruct((1, MOST, HW), BF16),
            jax.ShapeDtypeStruct((NX, EROWS, FB), BF16),
            jax.ShapeDtypeStruct((NX, EROWS, FB), BF16),
            jax.ShapeDtypeStruct((ROWS, 128), F32),
        ),
        in_specs=smem * 2 + hbm * 15 + vmem(6),
        out_specs=tuple(vmem(6)),
        scratch_shapes=[
            pltpu.VMEM((8, NZ, STRIP, 2 * HW), BF16),
            pltpu.VMEM((ROWS, 2 * HW), F32),
            pltpu.VMEM((ROWS, 2 * HW), BF16),
            pltpu.VMEM((ROWS, HW), BF16),
            pltpu.VMEM((ROWS, 128), F32),
            pltpu.VMEM((ROWS, 128), F32),
            pltpu.VMEM((ROWS, HW), BF16),
            pltpu.VMEM((ROWS, HW), BF16),
            pltpu.VMEM((8, EROWS, FB), BF16),
            pltpu.VMEM((8, ROWS, FB), BF16),
            pltpu.VMEM((ROWS, HW), BF16),
            pltpu.SemaphoreType.DMA((19,)),
            pltpu.SemaphoreType.DMA((8,)),
        ],
        compiler_params=pltpu.CompilerParams(vmem_limit_bytes=60 * 2**20),
        cost_estimate=pl.CostEstimate(flops=flops, bytes_accessed=20000000, transcendentals=100000),
        name="layer",
    )(place, facts, blocks, *a_pieces, *b_pieces, pick, *cot_pieces, q_gain, k_gain)


def pair_kernel(own, got, *outs):
    for k, out in enumerate(outs):
        out[:ROWS, :] = (own[k, :ROWS, :].astype(F32) + got[k, :ROWS, :].astype(F32)).astype(BF16)
        a, b = stats_of(own[k, ROWS:, :]), stats_of(got[k, ROWS:, :])
        out[ROWS:, :] = stat_rows(a[0] + b[0], a[1] + b[1])


def pair_sum(own, got):
    return pl.pallas_call(
        pair_kernel,
        out_shape=(jax.ShapeDtypeStruct((EROWS, FB), BF16),) * NX,
        in_specs=vmem(2),
        out_specs=tuple(vmem(NX)),
        compiler_params=pltpu.CompilerParams(vmem_limit_bytes=16 * 2**20),
        cost_estimate=pl.CostEstimate(flops=1000000, bytes_accessed=6000000, transcendentals=0),
        name="pair_sum",
    )(own, got)


def embed_back_kernel(
    place, own, r1, r2, r3, e_own, ms, pix, own_out, send_out, full
):
    y = place[1]
    part = own[:ROWS, :].astype(F32)
    sums = stats_of(own[ROWS:, :])
    for ref in (r1, r2, r3):
        part = part + ref[:ROWS, :].astype(F32)
        more = stats_of(ref[ROWS:, :])
        sums = (sums[0] + more[0], sums[1] + more[1])
    mean, scale = ms[:, 0:1], ms[:, 1:2]
    gain = gain_of(e_own[ROWS:, :])
    chooser = jnp.where(lax.broadcasted_iota(jnp.int32, (8, 128), 0) == 0, 1.0 / D, 0.0)
    columns = []
    for v in sums:
        tall = jnp.broadcast_to(v[:, :ROWS], (8, ROWS))
        columns.append(
            lax.dot_general(tall, chooser, TN, preferred_element_type=F32, precision=HIGH)[:, :1]
        )
    t = part * gain
    unit = (e_own[:ROWS, :].astype(F32) - mean) * scale
    grad = (scale * (t - columns[0] - unit * columns[1])).astype(BF16)
    full[...] = dot(grad, pix[...], TN)
    for k in range(NY):
        at = pl.multiple_of(lax.rem(y + k, NY) * YROWS, YROWS)
        piece = full[pl.ds(at, YROWS), :]
        if k == 0:
            own_out[...] = piece
        else:
            send_out[k - 1] = piece.astype(BF16)


def embed_back(place, *args):
    return pl.pallas_call(
        embed_back_kernel,
        out_shape=(
            jax.ShapeDtypeStruct((YROWS, PATCH), F32),
            jax.ShapeDtypeStruct((NY - 1, YROWS, PATCH), BF16),
        ),
        in_specs=[pl.BlockSpec(memory_space=pltpu.SMEM)] + vmem(7),
        out_specs=tuple(vmem(2)),
        scratch_shapes=[pltpu.VMEM((FB, PATCH), F32)],
        compiler_params=pltpu.CompilerParams(vmem_limit_bytes=32 * 2**20),
        cost_estimate=pl.CostEstimate(
            flops=2 * ROWS * FB * PATCH, bytes_accessed=5000000, transcendentals=0
        ),
        name="embed_back",
    )(place, *args)


def per_device(
    pixels,
    patch_counts,
    pack_index,
    embed_weight,
    norm_gain,
    query_weight,
    key_weight,
    query_gain,
    key_gain,
    cotangent,
):
    x, y, z, c = [lax.axis_index(name) for name in ("x", "y", "z", "core")]
    d = (y * NZ + z) * NC + c
    place = jnp.stack([x, y, z, c]).astype(jnp.int32)

    strip = jnp.swapaxes(embed_weight.reshape(PATCH, PIECE), 0, 1)
    strip = by_core(z % 2, strip, z_swap(strip, 1), 0)
    sent, kept, source = prep(
        place, patch_counts, pack_index, query_weight, key_weight, cotangent, pixels
    )
    got = core_swap(sent)
    n_w = 2 * NC * PIECE
    shards = []
    for k in range(2):
        rows = slice(k * n_w, (k + 1) * n_w)
        mine = kept[rows].reshape(NC, 2 * PIECE, HW)
        shards.append(by_core(c, mine, got[rows].reshape(NC, 2 * PIECE, HW), 1))
    a0, b0 = shards

    after = lax.optimization_barrier
    a_own = lax.all_gather(a0, "z", axis=0, tiled=False)
    b_near = [y_shift(b0, -k) for k in range(1, NY)]
    for step in (2, 4):
        strip = by_core(z // step % 2, strip, z_swap(strip, step), 0)
    strip, b_near = after((strip, b_near))
    b_own = in_order(place, [b0] + b_near)
    embed_pieces = [strip] + [y_shift(strip, -k) for k in range(1, NY)]
    bl1, br1 = z_shift(b_own, 1), z_shift(b_own, -1)
    bl2, br2 = z_shift(bl1, 1), z_shift(br1, -1)
    bl3, br3 = z_shift(bl2, 1), z_shift(br2, -1)
    bl4, br4 = z_shift(bl3[:4], 1), z_shift(br3[4:], -1)
    a_low, a_high = y_shift(a_own, 1), y_shift(a_own, -1)
    a_pieces = [a_own, a_low, a_high, y_shift(a_low[:4], 1), y_shift(a_high[4:], -1)]
    b_pieces = [b_own, bl1, br1, bl2, br2, bl3, br3, bl4, br4]

    gain_here = jnp.where(
        c == 0, norm_gain.reshape(-1, NC, PIECE)[:, 0], norm_gain.reshape(-1, NC, PIECE)[:, 1]
    ).reshape(1, FB)
    column = jnp.arange(HW, dtype=jnp.int32)[None, None, :]
    feature = (c * HC + column // HD) * (D // HEADS) + column % HD
    at = (feature // (NC * PIECE)) * PIECE + feature % PIECE
    part = (feature // PIECE) % NC
    pick = (
        (jnp.arange(FB, dtype=jnp.int32)[None, :, None] == at)
        & (jnp.arange(NC, dtype=jnp.int32)[:, None, None] == part)
    ).astype(BF16)
    source, pick = after((source, pick))
    e_own, pix, facts = embed(place, source, got, embed_pieces, gain_here)
    blocks = lax.all_gather(e_own, ("x", "core"), axis=0, tiled=False)

    kept_cot, got_cot, bl2 = after((kept[2 * n_w :], got[2 * n_w : 2 * n_w + PACK], bl2))
    packs = by_core(c, kept_cot[None], got_cot[None], 0)
    packs = packs.reshape(NC, REACH, MOST, HW)
    near = chip_shift(jnp.stack([packs[0, 1], packs[0, 2], packs[1, 2], packs[1, 3]]), -1)
    far = chip_shift(packs[0, 3], -2)

    att_here, att_near, att_far, own_grad, other_grad, ms = layer(
        place,
        facts,
        blocks,
        a_pieces,
        b_pieces,
        pick,
        (packs, near, far),
        query_gain.reshape(1, HD),
        key_gain.reshape(1, HD),
    )

    pair = pair_sum(own_grad, core_swap(other_grad))
    arrived = [x_shift(pair[k], k) for k in range(1, NX)]
    grad_own, grad_send = embed_back(place, pair[0], *arrived, e_own, ms, pix)
    total = grad_own
    for k in range(1, NY):
        total = total + y_shift(grad_send[k - 1], k).astype(F32)
    total = total.reshape(NZ, PIECE, PATCH)
    sent = total.astype(BF16)
    arrived = lax.all_to_all(sent, "z", 0, 0)
    embed_grad = jnp.sum(arrived.astype(F32), axis=0)
    embed_grad = jnp.swapaxes(embed_grad, 0, 1).reshape(PATCH, 1, PIECE)

    near = chip_shift(att_near, 1)
    far = chip_shift(att_far, 2)
    packs = jnp.concatenate(
        [att_here[0], near[2], near[0], far[0], att_here[2], att_here[1], near[3], near[1]], axis=0
    ).reshape(NC, PACK, HW)
    keep = jnp.where(c == 0, packs[0], packs[1])
    give = jnp.where(c == 0, packs[1], packs[0])
    attended = by_core(c, keep, core_swap(give), 1)
    return attended, embed_grad


def solution(mesh):
    chips = Mesh(mesh.devices.reshape(NY, NZ, NC, NX), ("y", "z", "core", "x"))
    dp = ("y", "z", "core")
    placed = (
        P(dp, None),
        P(dp),
        P(dp),
        P(None, "x", dp),
        P("x"),
        P(dp, "x"),
        P(dp, "x"),
        P(),
        P(),
        P(dp, "x"),
    )
    return jax.shard_map(
        per_device,
        mesh=chips,
        in_specs=placed,
        out_specs=(P(dp, "x"), P(None, "x", dp)),
        check_vma=False,
    )
```
